32 devices in a mesh: grp: 2 (over x), ep: 16 (over z, y, core).
Axes of the slice: x: 2, y: 2, z: 4, core: 2. Of those that a mesh axis runs over, the one named last changes fastest.
Arguments:
- queries: bfloat16 [1024, 4096], P(('grp', 'ep')), parts along dimension 0, may hold values from -6 to 6
- fresh_key_value: bfloat16 [1024, 2, 256], P(('grp', 'ep')), parts along dimension 0, may hold values from -4 to 4
- key_value_cache: bfloat16 [1024, 2, 256, 256], P(('grp', 'ep')), parts along dimension 0, may hold values from -6 to 6
- lengths: int32 [1024], P(('grp', 'ep')), parts along dimension 0, may hold values from 2 to 256, as said below
- hidden: bfloat16 [1024, 4096], P(('grp', 'ep')), parts along dimension 0, may hold values from -420 to 420
- expert_norm_gain: bfloat16 [4096], replicated, may hold values from 0.099609375 to 1.8984375
- routes: int32 [1024, 8], P(('grp', 'ep')), parts along dimension 0, may hold values from 0 to 15, all different within a row; in each aligned block of 32 rows (0 to 31, 32 to 63, ...) at most 16 rows name the same one
- router_scores: float32 [1024, 8], P(('grp', 'ep')), parts along dimension 0, may hold values from -360 to 360
- gate_up_quant_codes: int32 [16, 4096, 512], P('ep'), may hold values from 0 to 4095
- gate_up_code_scale: bfloat16 [16, 64, 1536], P('ep'), may hold values from 0.015625 to 0.0625
- down_quant_codes: int32 [16, 256, 4096], P('ep'), may hold values from 0 to 4095
- down_code_scale: bfloat16 [16, 12, 4096], P('ep'), may hold values from 0.035888672 to 0.14355469
- adapter_input_down: bfloat16 [16, 4096, 32], P('ep'), may hold values from -0.09375 to 0.09375
- adapter_input_up: bfloat16 [16, 2, 16, 768], P('ep'), may hold values from -0.375 to 0.375
- adapter_output_down: bfloat16 [16, 768, 16], P('ep'), may hold values from -0.21875 to 0.21875
- adapter_output_up: bfloat16 [16, 16, 4096], P('ep'), may hold values from -0.375 to 0.375
Outputs:
- context: bfloat16 [1024, 4096], P(('grp', 'ep')), parts along dimension 0
- expert_sum: bfloat16 [1024, 4096], P(('grp', 'ep')), parts along dimension 0
The draws below stay inside these ranges and needn't reach their ends.
There are 2 independent parts, one for each index of `grp`. The reference program is written for one: setup_inputs(seed, part) draws one part's arguments, and reference() takes and returns one part's arrays. A program takes and returns all parts, laid end to end along the dimension named above; an argument that names none is the same for every part. Nothing has to cross between parts.
Inputs may be any that keep to these rules, and one draw needn't show every extreme that they name: `routes`: each row names 8 different experts, and every expert is named by some row. Among the rows of one device, no expert is named more than 16 times, and in every draw some device's rows name some expert exactly 16 times. `lengths`: among the rows of each device, one row has length 256.
All inputs are finite; a program needn't handle non-finite values.
Results may differ from the reference program's by a relative error of at most 0.0081.
Values may be sent and summed in bfloat16 or wider, within the bound.
No kernel may reach another device: no remote copies, remote signals or barrier semaphores. Data moves between devices by JAX's collectives and lax.ppermute only.
A program may use at most 192 MiB of HBM per device.

```python
import math
import jax
import jax.numpy as jnp
import numpy as np
from jax import lax

MODEL_WIDTH = 4096
HEADS = 32
KV_HEADS = 2
HEAD = 128
HIDDEN_HALF = 768
QB = 64
ADAPTER_RANK = 16
TOPK = 8
ROWS = 32
CTX = 256
EXPERT_COUNT = 16
TOKENS = 512
CAP = 16
N_EP = 16


def draw_queries(key, part):
    key = jax.random.fold_in(key, 5)
    sample = jnp.clip(jax.random.normal(key, (TOKENS, HEADS * HEAD), jnp.float32), -4.0, 4.0)
    return sample.astype(jnp.bfloat16)


def draw_key_value_cache(key, part):
    key = jax.random.fold_in(key, 6)
    cache_shape = (TOKENS, 2, CTX, KV_HEADS * HEAD)
    sample = jnp.clip(jax.random.normal(key, cache_shape, jnp.float32), -4.0, 4.0)
    return sample.astype(jnp.bfloat16)


def draw_lengths(key, part):
    key = jax.random.fold_in(key, 7)
    subkeys = jax.random.split(key, 2)
    values = jax.random.randint(subkeys[0], (TOKENS,), 2, CTX + 1)
    full_spot = jax.random.randint(subkeys[1], (TOKENS // ROWS,), 0, ROWS)
    position = jnp.arange(TOKENS)
    return jnp.where(position % ROWS == full_spot[position // ROWS], CTX, values).astype(jnp.int32)


def draw_hidden(key, part):
    key = jax.random.fold_in(key, 8)
    subkeys = jax.random.split(key, 4)
    columns = jnp.exp(jax.random.uniform(subkeys[0], (MODEL_WIDTH,), jnp.float32, 0.0, 1.0) * math.log(10.0))
    row_scale = jnp.exp(jax.random.uniform(subkeys[1], (TOKENS,), jnp.float32, 0.0, 1.0) * math.log(10.0))
    sample = jnp.clip(jax.random.normal(subkeys[3], (TOKENS, MODEL_WIDTH), jnp.float32), -4.0, 4.0)
    return (sample * columns[None, :] * row_scale[:, None]).astype(jnp.bfloat16)


def draw_router_scores(key, part):
    key = jax.random.fold_in(key, 9)
    subkeys = jax.random.split(key, 1)
    sample = 2.0 * jnp.clip(jax.random.normal(subkeys[0], (TOKENS, TOPK), jnp.float32), -6.0, 6.0)
    return sample.astype(jnp.float32)


def plant(entries, rng, low, high):
    shape = entries.shape
    place = [jax.random.randint(jax.random.fold_in(rng, axis), (), 0, shape[axis]) for axis in range(len(shape))]
    entries = entries.at[tuple(place)].set(low)
    longest = shape.index(max(shape))
    place[longest] = (place[longest] + 1) % shape[longest]
    return entries.at[tuple(place)].set(high)


def shard_levels(own_key, dims, cuts, low, largest):
    gain = 1.0
    for dim, shards_of in cuts:
        heights = jax.random.uniform(jax.random.fold_in(jax.random.fold_in(own_key, 6), dim), (shards_of,), jnp.float32, low / len(cuts), largest / len(cuts))
        gain = gain * jnp.repeat(jnp.exp(heights), dims[dim] // shards_of).reshape((-1,) + (1,) * (len(dims) - 1 - dim))
    return gain


def routed_block(rng, own, number, rows, amount, top, bound, lean):
    ranking = jax.random.permutation(rng, amount)
    heavy_load, ordinary = load_shares(amount, rows * top, bound, lean, True), load_shares(amount, rows * top, bound, lean, False)
    places = jnp.arange(amount)

    def named(sizes, rotation):
        used = int((sizes > 0).sum())
        fixed = max(1, used // 4)
        shifted = fixed + (places - fixed + rotation * (used - fixed)) % max(1, amount - fixed)
        return jnp.zeros((amount,), jnp.int32).at[ranking[jnp.where(places < fixed, places, shifted)]].set(jnp.asarray(sizes, jnp.int32))

    sizes = jnp.where(number % 4 == 0, named(heavy_load, number // 4), named(ordinary, number - number // 4 - 1))
    mixed = jax.random.permutation(jax.random.fold_in(own, 3), amount)
    source_of, receiver = mixed[0:amount // 2 * 2:2], mixed[1:amount // 2 * 2:2]
    margin = jnp.minimum(sizes[source_of] - 1, bound - sizes[receiver]) // 2
    margin = jnp.where((source_of == ranking[0]) | (receiver == ranking[0]) | (sizes[receiver] == 0), 0, jnp.maximum(margin, 0))
    shifted = jax.random.randint(jax.random.fold_in(own, 4), (amount // 2,), 0, 1 << 20) % (margin + 1)
    sizes = sizes.at[source_of].add(-shifted).at[receiver].add(shifted)
    members = jnp.searchsorted(jnp.cumsum(sizes), jnp.arange(rows * top), side="right").astype(jnp.int32)
    listing = members.reshape(top, rows).T
    listing = listing[jax.random.permutation(jax.random.fold_in(own, 1), rows)]
    rotation = jax.random.randint(jax.random.fold_in(own, 2), (rows, 1), 0, top)
    return jnp.take_along_axis(listing, (jnp.arange(top)[None, :] + rotation) % top, axis=1)


def load_shares(number_of, total, limit, slope, full):
    loads = [(1 << 20) // math.isqrt(grade ** slope) + 1 for grade in range(1, number_of + 1)]
    largest = limit if full else min(limit, max(-(-total // number_of), total * loads[0] // sum(loads)))
    least = 1 if total - largest >= number_of - 1 else 0
    counts, spare = [largest] + [least] * (number_of - 1), total - largest - least * (number_of - 1)
    while spare > 0:
        free = [i for i in range(1, number_of) if counts[i] < largest] or [i for i in range(1, number_of) if counts[i] < limit]
        whole, left = sum([loads[i] for i in free]), spare
        for i in free:
            extra = min(limit - counts[i], max(1, left * loads[i] // whole), spare)
            counts[i] = counts[i] + extra
            spare = spare - extra
    return np.array(counts)


def normal_values(stream_key, extent, deviation, limit, cuts=(), kind=jnp.bfloat16):
    gain = shard_levels(stream_key, extent, cuts, -0.22, 0.18) if cuts else 1.0
    array = jax.random.normal(stream_key, extent, jnp.float32) * deviation * gain
    return jnp.minimum(jnp.maximum(array, -limit), limit).astype(kind)


def setup_inputs(seed: int = 0, part: int = 0) -> dict:
    arg_keys = jax.random.split(jax.random.key(seed), 17)
    part_splits = jax.random.split(jax.random.fold_in(arg_keys[16], part), 17)
    queries = draw_queries(jax.random.fold_in(jax.random.fold_in(arg_keys[16], part), 71), part)
    fresh_key_value = normal_values(part_splits[1], (TOKENS, 2, KV_HEADS * HEAD), 1.0, 4.0, ((0, 16),))
    key_value_cache = draw_key_value_cache(jax.random.fold_in(jax.random.fold_in(arg_keys[16], part), 71), part)
    lengths = draw_lengths(jax.random.fold_in(jax.random.fold_in(arg_keys[16], part), 71), part)
    hidden = draw_hidden(jax.random.fold_in(jax.random.fold_in(arg_keys[16], part), 71), part)
    expert_norm_gain = jnp.clip(1.0 + 0.18 * jax.random.normal(arg_keys[5], (MODEL_WIDTH,), jnp.float32), 0.099609375, 1.8984375).astype(jnp.bfloat16)
    routes_keys = jax.random.split(jax.random.fold_in(part_splits[6], 1), TOKENS // ROWS)
    routes_turns = jax.random.permutation(jax.random.fold_in(part_splits[6], 3), TOKENS // ROWS)
    routes = jax.vmap(lambda own, number: routed_block(jax.random.fold_in(part_splits[6], 2), own, number, ROWS, EXPERT_COUNT, TOPK, CAP, 2))(routes_keys, routes_turns).reshape((TOKENS, TOPK))
    router_scores = draw_router_scores(jax.random.fold_in(jax.random.fold_in(arg_keys[16], part), 71), part)
    gate_up_quant_codes = plant(jax.random.randint(arg_keys[8], (EXPERT_COUNT, MODEL_WIDTH, 2 * HIDDEN_HALF // 3), 0, 4096), jax.random.fold_in(arg_keys[8], 1), 0, 4095).astype(jnp.int32)
    gate_up_code_scale = jnp.clip(jnp.exp(math.log(0.0625) - 1.3862944 * jax.random.uniform(arg_keys[9], (EXPERT_COUNT, MODEL_WIDTH // QB, 2 * HIDDEN_HALF), jnp.float32) ** shard_levels(arg_keys[9], (EXPERT_COUNT, MODEL_WIDTH // QB, 2 * HIDDEN_HALF), ((0, 16),), -0.2, 0.2)), 0.015625, 0.0625).astype(jnp.bfloat16)
    down_quant_codes = plant(jax.random.randint(arg_keys[10], (EXPERT_COUNT, HIDDEN_HALF // 3, MODEL_WIDTH), 0, 4096), jax.random.fold_in(arg_keys[10], 1), 0, 4095).astype(jnp.int32)
    down_code_scale = jnp.clip(jnp.exp(math.log(0.14355469) - 1.3862944 * jax.random.uniform(arg_keys[11], (EXPERT_COUNT, HIDDEN_HALF // QB, MODEL_WIDTH), jnp.float32) ** shard_levels(arg_keys[11], (EXPERT_COUNT, HIDDEN_HALF // QB, MODEL_WIDTH), ((0, 16),), -0.2, 0.2)), 0.035888672, 0.14355469).astype(jnp.bfloat16)
    adapter_input_down = normal_values(arg_keys[12], (EXPERT_COUNT, MODEL_WIDTH, 2 * ADAPTER_RANK), MODEL_WIDTH ** -0.5, 0.09375, ((0, 16),))
    adapter_input_up = normal_values(arg_keys[13], (EXPERT_COUNT, 2, ADAPTER_RANK, HIDDEN_HALF), (16 * ADAPTER_RANK) ** -0.5, 0.375, ((0, 16),))
    adapter_output_down = normal_values(arg_keys[14], (EXPERT_COUNT, HIDDEN_HALF, ADAPTER_RANK), HIDDEN_HALF ** -0.5, 0.21875, ((0, 16),))
    adapter_output_up = normal_values(arg_keys[15], (EXPERT_COUNT, ADAPTER_RANK, MODEL_WIDTH), (16 * ADAPTER_RANK) ** -0.5, 0.375, ((0, 16),))
    return dict(queries=queries, fresh_key_value=fresh_key_value, key_value_cache=key_value_cache, lengths=lengths, hidden=hidden, expert_norm_gain=expert_norm_gain, routes=routes, router_scores=router_scores, gate_up_quant_codes=gate_up_quant_codes, gate_up_code_scale=gate_up_code_scale, down_quant_codes=down_quant_codes, down_code_scale=down_code_scale, adapter_input_down=adapter_input_down, adapter_input_up=adapter_input_up, adapter_output_down=adapter_output_down, adapter_output_up=adapter_output_up)


code_levels = (-1.0, -0.6961928009986877, -0.5250730514526367, -0.39491748809814453, -0.28444138169288635, -0.18477343022823334, -0.09105003625154495, 0.0, 0.07958029955625534, 0.16093020141124725, 0.24611230194568634, 0.33791524171829224, 0.44070982933044434, 0.5626170039176941, 0.7229568362236023, 1.0)
adapter_scale = 2.0
norm_epsilon = 1e-06

def decode_levels(nibbles):
    decoded = jnp.zeros(nibbles.shape, jnp.float32)
    for code_index in range(16):
        decoded = jnp.where(nibbles == code_index, jnp.float32(code_levels[code_index]), decoded)
    return decoded

def unpack_columns(packed):
    nibbles = [jnp.bitwise_and(jnp.right_shift(packed, 4 * nibble_pos), 15) for nibble_pos in range(3)]
    return jnp.concatenate(nibbles, axis=1)

def unpack_rows(packed):
    nibbles = [jnp.bitwise_and(jnp.right_shift(packed, 4 * nibble_pos), 15) for nibble_pos in range(3)]
    return jnp.concatenate(nibbles, axis=0)

def dequantize(nibbles, block_scale):
    levels = decode_levels(nibbles)
    blocks = block_scale.shape[0]
    columns = levels.shape[1]
    shaped = levels.reshape(blocks, levels.shape[0] // blocks, columns) * block_scale.astype(jnp.float32)[:, None, :]
    return shaped.reshape(levels.shape[0], columns).astype(jnp.bfloat16)

def expert_rows(expert_in, weight_both, down_weight_matrix, enter_a, enter_up_map, leave_a, leave_up_map):
    hidden_units_width = down_weight_matrix.shape[0]
    low_rank_term = leave_a.shape[1]
    middle_hidden = jnp.dot(expert_in, enter_a, preferred_element_type=jnp.float32).astype(jnp.bfloat16)
    joined_output = jnp.dot(expert_in, weight_both, preferred_element_type=jnp.float32)
    gate_values = joined_output[:, :hidden_units_width] + adapter_scale * jnp.dot(middle_hidden[:, :low_rank_term], enter_up_map[0], preferred_element_type=jnp.float32)
    upward_hidden = joined_output[:, hidden_units_width:] + adapter_scale * jnp.dot(middle_hidden[:, low_rank_term:], enter_up_map[1], preferred_element_type=jnp.float32)
    active_rows = (jax.nn.silu(gate_values) * upward_hidden).astype(jnp.bfloat16)
    lowered_hidden = jnp.dot(active_rows, leave_a, preferred_element_type=jnp.float32).astype(jnp.bfloat16)
    final_output = jnp.dot(active_rows, down_weight_matrix, preferred_element_type=jnp.float32) + adapter_scale * jnp.dot(lowered_hidden, leave_up_map, preferred_element_type=jnp.float32)
    return final_output.astype(jnp.bfloat16)

def attend(queries, fresh_key_value, key_value_cache, lengths):
    row_count = queries.shape[0]
    per_group = HEADS // KV_HEADS
    query_view = queries.astype(jnp.float32).reshape(row_count, KV_HEADS, per_group, HEAD)
    cache_view = key_value_cache.astype(jnp.float32).reshape(row_count, 2, CTX, KV_HEADS, HEAD)
    fresh_view = fresh_key_value.astype(jnp.float32).reshape(row_count, 2, KV_HEADS, HEAD)
    scaling = 1.0 / math.sqrt(HEAD)
    old_scores = jnp.einsum('tgqd,tcgd->tgqc', query_view, cache_view[:, 0]) * scaling
    new_scores = jnp.einsum('tgqd,tgd->tgq', query_view, fresh_view[:, 0]) * scaling
    visible = jnp.arange(CTX)[None, :] < lengths[:, None]
    old_scores = jnp.where(visible[:, None, None, :], old_scores, -jnp.inf)
    highest = jnp.maximum(lax.optimization_barrier(jnp.max(old_scores, axis=-1)), new_scores)
    old_exp = jnp.exp(old_scores - highest[..., None])
    new_exp = jnp.exp(new_scores - highest)
    denominator = lax.optimization_barrier(jnp.sum(old_exp, axis=-1)) + new_exp
    old_prob = (old_exp / denominator[..., None]).astype(jnp.bfloat16)
    new_prob = (new_exp / denominator).astype(jnp.bfloat16)
    blended = jnp.einsum('tgqc,tcgd->tgqd', old_prob.astype(jnp.float32), cache_view[:, 1])
    blended = blended + new_prob.astype(jnp.float32)[..., None] * fresh_view[:, 1][:, :, None, :]
    return blended.reshape(row_count, HEADS * HEAD).astype(jnp.bfloat16)

def reference(queries, fresh_key_value, key_value_cache, lengths, hidden, expert_norm_gain, routes, router_scores, gate_up_quant_codes, gate_up_code_scale, down_quant_codes, down_code_scale, adapter_input_down, adapter_input_up, adapter_output_down, adapter_output_up):
    context = attend(queries, fresh_key_value, key_value_cache, lengths)
    hidden_wide = hidden.astype(jnp.float32)
    spread = lax.optimization_barrier(jnp.mean(hidden_wide * hidden_wide, axis=-1, keepdims=True))
    normed = (hidden_wide * lax.rsqrt(spread + norm_epsilon) * expert_norm_gain.astype(jnp.float32)).astype(jnp.bfloat16)
    shares = jax.nn.softmax(router_scores, axis=-1)
    token_count = hidden.shape[0]
    slot_limit = min(token_count, N_EP * CAP)

    def single_expert(summed_output, inputs):
        expert, codes_both, scale_both, codes_down, scale_down, enter_a, enter_up_map, leave_a, leave_up_map = inputs
        weight_both = dequantize(unpack_columns(codes_both), scale_both)
        down_weight_matrix = dequantize(unpack_rows(codes_down), scale_down)
        chosen = routes == expert
        weight = lax.optimization_barrier(jnp.sum(jnp.where(chosen, shares, 0.0), axis=-1))
        picked = jnp.any(chosen, axis=-1)
        live_count = jnp.sum(picked.astype(jnp.int32))
        where_rows, = jnp.nonzero(picked, size=slot_limit, fill_value=0)
        where_rows = where_rows.astype(jnp.int32)
        final_output = expert_rows(normed[where_rows], weight_both, down_weight_matrix, enter_a, enter_up_map, leave_a, leave_up_map)
        live_slot = jnp.arange(slot_limit) < live_count
        scaled = jnp.where(live_slot[:, None], weight[where_rows][:, None] * final_output.astype(jnp.float32), 0.0)
        return (summed_output.at[where_rows].add(scaled), None)
    start_index = jnp.zeros((token_count, MODEL_WIDTH), jnp.float32)
    summed_output, unused_value = lax.scan(single_expert, start_index, (jnp.arange(EXPERT_COUNT, dtype=jnp.int32), gate_up_quant_codes, gate_up_code_scale, down_quant_codes, down_code_scale, adapter_input_down, adapter_input_up, adapter_output_down, adapter_output_up))
    return (context, summed_output.astype(jnp.bfloat16))
```

```python
import functools
import math

import jax
import jax.numpy as jnp
from jax import lax
from jax.experimental import pallas as pl
from jax.experimental.pallas import tpu as pltpu
from jax.sharding import PartitionSpec as P

HEADS = 32
KV_HEADS = 2
HEAD = 128
RANK = 16
LANES = 128
GROUP = 64
code_levels = (
    -1.0,
    -0.6961928009986877,
    -0.5250730514526367,
    -0.39491748809814453,
    -0.28444138169288635,
    -0.18477343022823334,
    -0.09105003625154495,
    0.0,
    0.07958029955625534,
    0.16093020141124725,
    0.24611230194568634,
    0.33791524171829224,
    0.44070982933044434,
    0.5626170039176941,
    0.7229568362236023,
    1.0,
)
adapter_scale = 2.0
norm_epsilon = 1e-06
f32 = jnp.float32
bf16 = jnp.bfloat16


def params(mib):
    return pltpu.CompilerParams(vmem_limit_bytes=mib * 2**20)


def whole(shape):
    return pl.BlockSpec(shape, lambda *_: (0,) * len(shape))


def norm_kernel(hidden, gain, routes, scores, out):
    width = hidden.shape[1]
    wide = hidden[...].astype(f32)
    spread = jnp.mean(wide * wide, axis=-1, keepdims=True)
    normed = wide * lax.rsqrt(spread + norm_epsilon) * gain[...].astype(f32)
    out[:, :width] = normed.astype(bf16)
    logits = scores[...]
    parts = jnp.exp(logits - jnp.max(logits, axis=-1, keepdims=True))
    shares = parts / jnp.sum(parts, axis=-1, keepdims=True)
    lane = lax.broadcasted_iota(jnp.int32, (hidden.shape[0], LANES), 1)
    expert = lane & (LANES // 2 - 1)
    table = jnp.zeros(expert.shape, f32)
    for k in range(routes.shape[1]):
        table = table + jnp.where(routes[:, k : k + 1] == expert, shares[:, k : k + 1], 0.0)
    high = table.astype(bf16)
    low = (table - high.astype(f32)).astype(bf16)
    out[:, width:] = jnp.where(lane < LANES // 2, high.astype(f32), low.astype(f32)).astype(bf16)


def norm_rows(hidden, gain, routes, scores):
    rows, width = hidden.shape
    return pl.pallas_call(
        norm_kernel,
        out_shape=jax.ShapeDtypeStruct((rows, width + LANES), bf16),
        compiler_params=params(16),
    )(hidden, gain.reshape(1, width), routes, scores)


def level_tables():
    sub = lax.broadcasted_iota(jnp.int32, (8, LANES), 0)
    low = jnp.zeros((8, LANES), f32)
    high = low
    for i in range(8):
        low = jnp.where(sub == i, code_levels[i], low)
        high = jnp.where(sub == i, code_levels[i + 8], high)
    return low, high


def decode(tables, words, nibble):
    pieces = []
    for q in range(words.shape[0] // 8):
        word = words[8 * q : 8 * q + 8]
        entry = (word >> (4 * nibble)) & 7
        upper = (word & (8 << (4 * nibble))) != 0
        low = jnp.take_along_axis(tables[0], entry, axis=0, mode="promise_in_bounds")
        high = jnp.take_along_axis(tables[1], entry, axis=0, mode="promise_in_bounds")
        pieces.append(jnp.where(upper, high, low))
    return jnp.concatenate(pieces, axis=0)


def enter_kernel(codes, scale, down_map, up_map, out):
    tables = level_tables()
    rows, third = codes.shape
    half = out.shape[0] * LANES
    for tile in range(out.shape[0]):
        adapter = jnp.dot(down_map[...], up_map[tile], preferred_element_type=f32)
        for side in range(2):
            column = side * half + tile * LANES
            nibble, offset = divmod(column, third)
            for g in range(rows // GROUP):
                words = codes[pl.ds(g * GROUP, GROUP), pl.ds(offset, LANES)]
                factor = scale[0, pl.ds(g, 1), pl.ds(column, LANES)].astype(f32)
                value = decode(tables, words, nibble) * factor
                value = value + adapter[g * GROUP : (g + 1) * GROUP, side * LANES : (side + 1) * LANES]
                out[tile, pl.ds(g * GROUP, GROUP), pl.ds(side * LANES, LANES)] = value.astype(bf16)


def enter_weights(codes, scale, down_map, up_map, block=512):
    width, third = codes.shape
    columns = 3 * third
    half = columns // 2
    tiles = half // LANES
    wide = (adapter_scale * up_map.astype(f32)).astype(bf16).reshape(2, RANK, tiles, LANES)
    spread = jnp.zeros((tiles, 2, RANK, 2, LANES), bf16)
    spread = spread.at[:, 0, :, 0].set(wide[0].transpose(1, 0, 2))
    spread = spread.at[:, 1, :, 1].set(wide[1].transpose(1, 0, 2))
    spread = spread.reshape(tiles, 2 * RANK, 2 * LANES)
    return pl.pallas_call(
        enter_kernel,
        grid=(width // block,),
        in_specs=[
            pl.BlockSpec((block, third), lambda i: (i, 0)),
            pl.BlockSpec((1, block // GROUP, columns), lambda i: (i, 0, 0)),
            pl.BlockSpec((block, 2 * RANK), lambda i: (i, 0)),
            whole(spread.shape),
        ],
        out_specs=pl.BlockSpec((tiles, block, 2 * LANES), lambda i: (0, i, 0)),
        out_shape=jax.ShapeDtypeStruct((tiles, width, 2 * LANES), bf16),
        compiler_params=params(40),
        cost_estimate=pl.CostEstimate(flops=4 * 10**9, bytes_accessed=40 * 10**6, transcendentals=0),
    )(codes, scale.reshape(width // block, block // GROUP, columns), down_map, spread)


def leave_kernel(codes, scale, down_map, up_map, out):
    tables = level_tables()
    rows, columns = codes.shape
    adapter = jnp.dot(down_map[...], up_map[...], preferred_element_type=f32) * adapter_scale
    for j in range(columns // LANES):
        lanes = pl.ds(j * LANES, LANES)
        for nibble in range(3):
            for g in range(rows // GROUP):
                row = nibble * rows + g * GROUP
                words = codes[pl.ds(g * GROUP, GROUP), lanes]
                factor = scale[pl.ds(row // GROUP, 1), lanes].astype(f32)
                value = decode(tables, words, nibble) * factor
                value = value + adapter[row : row + GROUP, j * LANES : (j + 1) * LANES]
                out[pl.ds(row, GROUP), lanes] = value.astype(bf16)


def leave_weights(codes, scale, down_map, up_map, block=512):
    third, width = codes.shape
    rows = 3 * third
    return pl.pallas_call(
        leave_kernel,
        grid=(width // block,),
        in_specs=[
            pl.BlockSpec((third, block), lambda i: (0, i)),
            pl.BlockSpec((rows // GROUP, block), lambda i: (0, i)),
            whole((rows, RANK)),
            pl.BlockSpec((RANK, block), lambda i: (0, i)),
        ],
        out_specs=pl.BlockSpec((rows, block), lambda i: (0, i)),
        out_shape=jax.ShapeDtypeStruct((rows, width), bf16),
        compiler_params=params(40),
        cost_estimate=pl.CostEstimate(flops=2 * 10**9, bytes_accessed=20 * 10**6, transcendentals=0),
    )(codes, scale, down_map, up_map)


def expert_kernel(count, tiles, own, *refs):
    blocks = refs[:count]
    enter, leave = refs[count : count + 2]
    outs = refs[count + 2 : 2 * count + 2]
    rows_all, weight, active = refs[2 * count + 2 :]
    step = pl.program_id(0)
    rows = blocks[0].shape[0]
    width = rows_all.shape[1]

    @pl.when(step == 0)
    def _():
        lane = lax.broadcasted_iota(jnp.int32, (rows, LANES), 1)
        mine = (lane & (LANES // 2 - 1)) == own[0]
        for b in range(count):
            here = pl.ds(b * rows, rows)
            rows_all[here, :] = blocks[b][:, :width]
            table = jnp.where(mine, blocks[b][:, width:].astype(f32), 0.0)
            weight[here, :] = jnp.broadcast_to(jnp.sum(table, axis=-1, keepdims=True), (rows, LANES))

    @pl.when(step < tiles)
    def _():
        joined = jnp.dot(rows_all[...], enter[0], preferred_element_type=f32)
        gate = joined[:, :LANES]
        value = gate / (1.0 + jnp.exp(-gate)) * joined[:, LANES:]
        active[step] = value.astype(bf16)

    @pl.when(step >= tiles)
    def _():
        entry = jnp.concatenate([active[t] for t in range(tiles)], axis=1)
        for n in range(leave.shape[1] // 256):
            lanes = pl.ds(n * 256, 256)
            result = jnp.dot(entry, leave[:, lanes], preferred_element_type=f32)
            factor = jnp.concatenate([weight[...], weight[...]], axis=1)
            result = (result * factor).astype(bf16)
            for b in range(count):
                outs[b][:, lanes] = result[b * rows : (b + 1) * rows]


def expert(own, blocks, enter, leave, column_block=1024):
    count = len(blocks)
    rows, padded = blocks[0].shape
    width = padded - LANES
    tiles = enter.shape[0]
    steps = width // column_block
    total = count * rows
    return pl.pallas_call(
        functools.partial(expert_kernel, count, tiles),
        grid=(tiles + steps,),
        in_specs=[pl.BlockSpec(memory_space=pltpu.SMEM)]
        + [whole((rows, padded))] * count
        + [
            pl.BlockSpec((1, width, 2 * LANES), lambda i: (jnp.minimum(i, tiles - 1), 0, 0)),
            pl.BlockSpec((leave.shape[0], column_block), lambda i: (0, jnp.maximum(i - tiles, 0))),
        ],
        out_specs=[pl.BlockSpec((rows, column_block), lambda i: (0, jnp.maximum(i - tiles, 0)))] * count,
        out_shape=[jax.ShapeDtypeStruct((rows, width), bf16)] * count,
        scratch_shapes=[
            pltpu.VMEM((total, width), bf16),
            pltpu.VMEM((total, LANES), f32),
            pltpu.VMEM((tiles, total, LANES), bf16),
        ],
        compiler_params=params(50),
        cost_estimate=pl.CostEstimate(flops=10**10, bytes_accessed=28 * 10**6, transcendentals=0),
    )(own, *blocks, enter, leave)


def attend_kernel(lengths, queries, fresh, cache, out):
    first = pl.program_id(0) * queries.shape[0]
    scaling = 1.0 / math.sqrt(HEAD)
    positions = cache.shape[2]
    head = lax.broadcasted_iota(jnp.int32, (HEADS, HEAD), 0)
    upper = head < HEADS // KV_HEADS
    place = lax.broadcasted_iota(jnp.int32, (HEADS, positions), 1)
    for t in range(queries.shape[0]):
        query = queries[t]
        zero = jnp.zeros_like(query)
        spread = jnp.concatenate([jnp.where(upper, query, zero), jnp.where(upper, zero, query)], axis=1)
        old = lax.dot_general(
            spread, cache[t, 0], (((1,), (1,)), ((), ())), preferred_element_type=f32
        ) * scaling
        old = jnp.where(place < lengths[first + t], old, -jnp.inf)
        new_key = fresh[t, 0:1, :].astype(f32)
        new = jnp.sum(spread.astype(f32) * new_key, axis=-1, keepdims=True) * scaling
        highest = jnp.maximum(jnp.max(old, axis=-1, keepdims=True), new)
        old_exp = jnp.exp(old - highest)
        new_exp = jnp.exp(new - highest)
        denominator = jnp.sum(old_exp, axis=-1, keepdims=True) + new_exp
        old_prob = (old_exp / denominator).astype(bf16)
        new_prob = (new_exp / denominator).astype(bf16).astype(f32)
        blended = jnp.dot(old_prob, cache[t, 1], preferred_element_type=f32)
        blended = blended + new_prob * fresh[t, 1:2, :].astype(f32)
        out[t] = jnp.where(upper, blended[:, :HEAD], blended[:, HEAD:]).astype(bf16)


def attend(queries, fresh_key_value, key_value_cache, lengths, block=8):
    rows = queries.shape[0]
    positions, width = key_value_cache.shape[2:]
    context = pl.pallas_call(
        attend_kernel,
        grid_spec=pltpu.PrefetchScalarGridSpec(
            num_scalar_prefetch=1,
            grid=(rows // block,),
            in_specs=[
                pl.BlockSpec((block, HEADS, HEAD), lambda i, _: (i, 0, 0)),
                pl.BlockSpec((block, 2, width), lambda i, _: (i, 0, 0)),
                pl.BlockSpec((block, 2, positions, width), lambda i, _: (i, 0, 0, 0)),
            ],
            out_specs=pl.BlockSpec((block, HEADS, HEAD), lambda i, _: (i, 0, 0)),
        ),
        out_shape=jax.ShapeDtypeStruct((rows, HEADS, HEAD), bf16),
        compiler_params=params(32),
        cost_estimate=pl.CostEstimate(flops=5 * 10**8, bytes_accessed=20 * 10**6, transcendentals=0),
    )(lengths, queries.reshape(rows, HEADS, HEAD), fresh_key_value, key_value_cache)
    return context.reshape(rows, HEADS * HEAD)


def swap(value, bit):
    count = lax.axis_size("ep")
    return lax.ppermute(value, "ep", [(i, i ^ bit) for i in range(count)])


def add(terms):
    return sum(term.astype(f32) for term in terms[1:]) + terms[0].astype(f32)


def shards(
    queries,
    fresh_key_value,
    key_value_cache,
    lengths,
    hidden,
    expert_norm_gain,
    routes,
    router_scores,
    gate_up_quant_codes,
    gate_up_code_scale,
    down_quant_codes,
    down_code_scale,
    adapter_input_down,
    adapter_input_up,
    adapter_output_down,
    adapter_output_up,
):
    count = lax.axis_size("ep")
    bits = [1 << b for b in range(count.bit_length() - 1)]
    blocks = {0: norm_rows(hidden, expert_norm_gain, routes, router_scores)}
    for bit in reversed(bits):
        for r in list(blocks):
            blocks[r | bit] = swap(blocks[r], bit)
    enter = enter_weights(
        gate_up_quant_codes[0], gate_up_code_scale[0], adapter_input_down[0], adapter_input_up[0]
    )
    leave = leave_weights(
        down_quant_codes[0], down_code_scale[0], adapter_output_down[0], adapter_output_up[0]
    )
    own = lax.axis_index("ep").astype(jnp.int32).reshape(1)
    produced = expert(own, [blocks[r] for r in range(count)], enter, leave)
    sums = {r: [produced[r]] for r in range(count)}
    for bit in bits:
        for r in sorted(sums, reverse=True):
            if r & bit:
                sums[r ^ bit].append(swap(add(sums.pop(r)).astype(bf16), bit))
    context = attend(queries, fresh_key_value, key_value_cache, lengths)
    return (context, add(sums[0]).astype(bf16))


def solution(mesh):
    return jax.shard_map(
        shards,
        mesh=mesh,
        in_specs=(
            P(("grp", "ep"), None),
            P(("grp", "ep"), None, None),
            P(("grp", "ep"), None, None, None),
            P(("grp", "ep")),
            P(("grp", "ep"), None),
            P(),
            P(("grp", "ep"), None),
            P(("grp", "ep"), None),
            P("ep", None, None),
            P("ep", None, None),
            P("ep", None, None),
            P("ep", None, None),
            P("ep", None, None),
            P("ep", None, None, None),
            P("ep", None, None),
            P("ep", None, None),
        ),
        out_specs=(P(("grp", "ep"), None), P(("grp", "ep"), None)),
        check_vma=False,
    )
```

```python
import functools
import math

import jax
import jax.numpy as jnp
from jax import lax
from jax.experimental import pallas as pl
from jax.experimental.pallas import tpu as pltpu
from jax.sharding import PartitionSpec as P

HEADS = 32
KV_HEADS = 2
HEAD = 128
RANK = 16
LANES = 128
GROUP = 64
BLOCK = 512
code_levels = (
    -1.0,
    -0.6961928009986877,
    -0.5250730514526367,
    -0.39491748809814453,
    -0.28444138169288635,
    -0.18477343022823334,
    -0.09105003625154495,
    0.0,
    0.07958029955625534,
    0.16093020141124725,
    0.24611230194568634,
    0.33791524171829224,
    0.44070982933044434,
    0.5626170039176941,
    0.7229568362236023,
    1.0,
)
adapter_scale = 2.0
norm_epsilon = 1e-06
f32 = jnp.float32
bf16 = jnp.bfloat16


def params(mib):
    return pltpu.CompilerParams(vmem_limit_bytes=mib * 2**20)


def whole(shape):
    return pl.BlockSpec(shape, lambda *_: (0,) * len(shape))


def norm_kernel(hidden, gain, routes, scores, out):
    rows, width = hidden.shape
    wide = hidden[...].astype(f32)
    spread = jnp.mean(wide * wide, axis=-1, keepdims=True)
    normed = wide * lax.rsqrt(spread + norm_epsilon) * gain[...].astype(f32).reshape(1, width)
    out[:, :width] = normed.astype(bf16)
    logits = scores[...]
    parts = jnp.exp(logits - jnp.max(logits, axis=0, keepdims=True))
    shares = parts / jnp.sum(parts, axis=0, keepdims=True)
    place = lax.broadcasted_iota(jnp.int32, (LANES, rows), 0)
    named = place & (LANES // 2 - 1)
    table = jnp.zeros((LANES, rows), f32)
    for k in range(routes.shape[0]):
        table = table + jnp.where(routes[k : k + 1, :] == named, shares[k : k + 1, :], 0.0)
    high = table.astype(bf16).astype(f32)
    both = jnp.where(place < LANES // 2, high, table - high).astype(bf16)
    out[:, width:] = lax.dot_general(
        unit(rows), both, (((1,), (1,)), ((), ())), preferred_element_type=f32
    ).astype(bf16)


def unit(size):
    row = lax.broadcasted_iota(jnp.int32, (size, size), 0)
    return (row == lax.broadcasted_iota(jnp.int32, (size, size), 1)).astype(f32).astype(bf16)


def norm_rows(hidden, gain, routes, scores):
    rows, width = hidden.shape
    top = routes.shape[1]
    return pl.pallas_call(
        norm_kernel,
        grid=(1,),
        in_specs=[whole((rows, width)), whole((width,)), whole((top, rows)), whole((top, rows))],
        out_specs=whole((rows, width + LANES)),
        out_shape=jax.ShapeDtypeStruct((rows, width + LANES), bf16),
        compiler_params=params(56),
    )(hidden, gain, routes.T, scores.T)


def level_tables():
    sub = lax.broadcasted_iota(jnp.int32, (8, LANES), 0)
    low = jnp.zeros((8, LANES), f32)
    high = low
    for i in range(8):
        low = jnp.where(sub == i, code_levels[i], low)
        high = jnp.where(sub == i, code_levels[i + 8], high)
    return low, high


def decode(tables, words, nibble):
    pieces = []
    for q in range(words.shape[0] // 8):
        word = words[8 * q : 8 * q + 8]
        entry = (word >> (4 * nibble)) & 7
        upper = (word & (8 << (4 * nibble))) != 0
        low = jnp.take_along_axis(tables[0], entry, axis=0, mode="promise_in_bounds")
        high = jnp.take_along_axis(tables[1], entry, axis=0, mode="promise_in_bounds")
        pieces.append(jnp.where(upper, high, low))
    return jnp.concatenate(pieces, axis=0)


def copy(source, target, sem):
    move = pltpu.make_async_copy(source, target, sem)
    move.start()
    return move


def enter_kernel(
    part, codes, scale, down_map, up_map, before, out, made,
    words_of, scale_of, factors, down_of, up_of, spread, weights, small_sem, in_sem, out_sem,
):
    tiles, rows, _ = out.shape
    third = codes.shape[2]
    half = tiles * LANES
    first = part * rows
    blocks = rows // BLOCK
    arriving = [
        copy(scale.at[0, pl.ds(first // GROUP, rows // GROUP)], scale_of, small_sem.at[0]),
        copy(down_map.at[:, pl.ds(first, rows)], down_of, small_sem.at[1]),
        copy(up_map.at[0], up_of, small_sem.at[2]),
    ]

    def arriving_words(k):
        here = pl.multiple_of(k * BLOCK, BLOCK)
        return pltpu.make_async_copy(
            codes.at[0, pl.ds(first + here, BLOCK)], words_of.at[pl.ds(here, BLOCK)], in_sem.at[k]
        )

    for k in range(blocks):
        arriving_words(k).start()
    made[...] = jnp.zeros_like(made)
    tables = level_tables()
    spread[...] = jnp.zeros_like(spread)
    for move in arriving:
        move.wait()
    for tile in range(tiles):
        for side in range(2):
            piece = up_of[side, :, tile * LANES : (tile + 1) * LANES].astype(f32) * adapter_scale
            spread[tile, side * RANK : (side + 1) * RANK, side * LANES : (side + 1) * LANES] = piece.astype(bf16)
    factors[...] = scale_of[...].astype(f32)
    scales = BLOCK // GROUP

    def leaving(k):
        here = pl.ds(pl.multiple_of(k * BLOCK, BLOCK), BLOCK)
        return pltpu.make_async_copy(weights.at[:, here], out.at[:, here], out_sem.at[k])

    @pl.loop(0, blocks)
    def _(k):
        arriving_words(k).wait()
        here = pl.multiple_of(k * BLOCK, BLOCK)
        for tile in range(tiles):
            adapter = lax.dot_general(
                down_of[:, pl.ds(here, BLOCK)],
                spread[tile],
                (((0,), (0,)), ((), ())),
                preferred_element_type=f32,
            )
            for side in range(2):
                column = side * half + tile * LANES
                nibble, offset = divmod(column, third)
                factor = factors[pl.ds(pl.multiple_of(k * scales, scales), scales), pl.ds(column, LANES)]
                for g in range(scales):
                    packed = words_of[pl.ds(here + g * GROUP, GROUP), pl.ds(offset, LANES)]
                    value = decode(tables, packed, nibble) * factor[g : g + 1]
                    value = value + adapter[g * GROUP : (g + 1) * GROUP, side * LANES : (side + 1) * LANES]
                    weights[tile, pl.ds(here + g * GROUP, GROUP), pl.ds(side * LANES, LANES)] = value.astype(bf16)
        leaving(k).start()

    @pl.loop(0, blocks)
    def _(k):
        leaving(k).wait()


def in_hbm(count):
    return [pl.BlockSpec(memory_space=pltpu.HBM)] * count


def enter_weights(part, parts, codes, scale, down_map, up_map, before):
    _, width, third = codes.shape
    tiles = 3 * third // 2 // LANES
    rows = width // parts
    return pl.pallas_call(
        functools.partial(enter_kernel, part),
        in_specs=in_hbm(4) + [pl.BlockSpec(memory_space=pl.ANY)],
        out_specs=in_hbm(1) + [pl.BlockSpec(memory_space=pltpu.VMEM)],
        out_shape=[
            jax.ShapeDtypeStruct((tiles, rows, 2 * LANES), bf16),
            jax.ShapeDtypeStruct((8, LANES), f32),
        ],
        scratch_shapes=[
            pltpu.VMEM((rows, third), jnp.int32),
            pltpu.VMEM((rows // GROUP, 3 * third), bf16),
            pltpu.VMEM((rows // GROUP, 3 * third), f32),
            pltpu.VMEM((2 * RANK, rows), bf16),
            pltpu.VMEM(up_map.shape[1:], bf16),
            pltpu.VMEM((tiles, 2 * RANK, 2 * LANES), bf16),
            pltpu.VMEM((tiles, rows, 2 * LANES), bf16),
            pltpu.SemaphoreType.DMA((3,)),
            pltpu.SemaphoreType.DMA((rows // BLOCK,)),
            pltpu.SemaphoreType.DMA((rows // BLOCK,)),
        ],
        compiler_params=params(58),
        cost_estimate=pl.CostEstimate(flops=4 * 10**9, bytes_accessed=20 * 10**6, transcendentals=0),
    )(codes, scale, down_map[0].T, up_map, before)


def leave_kernel(
    codes, scale, down_map, up_map, before, out, made,
    words_of, scale_of, down_of, up_of, weights, small_sem, in_sem, out_sem,
):
    _, rows, columns = codes.shape
    arriving = [
        copy(scale.at[0], scale_of, small_sem.at[0]),
        copy(down_map, down_of, small_sem.at[1]),
        copy(up_map.at[0], up_of, small_sem.at[2]),
    ]
    blocks = columns // BLOCK

    def wide(k):
        return pl.ds(pl.multiple_of(k * BLOCK, BLOCK), BLOCK)

    def arriving_words(k):
        return pltpu.make_async_copy(codes.at[0, :, wide(k)], words_of.at[:, wide(k)], in_sem.at[k])

    def leaving(k):
        return pltpu.make_async_copy(weights.at[:, wide(k)], out.at[:, wide(k)], out_sem.at[k])

    for k in range(blocks):
        arriving_words(k).start()
    made[...] = jnp.zeros_like(made)
    tables = level_tables()
    for move in arriving:
        move.wait()

    @pl.loop(0, blocks)
    def _(k):
        arriving_words(k).wait()
        adapter = lax.dot_general(
            down_of[...], up_of[:, wide(k)], (((0,), (0,)), ((), ())), preferred_element_type=f32
        ) * adapter_scale
        for j in range(BLOCK // LANES):
            lanes = pl.ds(pl.multiple_of(k * BLOCK, BLOCK) + j * LANES, LANES)
            for nibble in range(3):
                for g in range(rows // GROUP):
                    row = nibble * rows + g * GROUP
                    packed = words_of[pl.ds(g * GROUP, GROUP), lanes]
                    factor = scale_of[pl.ds(row // GROUP, 1), lanes].astype(f32)
                    value = decode(tables, packed, nibble) * factor
                    value = value + adapter[row : row + GROUP, j * LANES : (j + 1) * LANES]
                    weights[pl.ds(row, GROUP), lanes] = value.astype(bf16)
        leaving(k).start()

    @pl.loop(0, blocks)
    def _(k):
        leaving(k).wait()


def leave_weights(codes, scale, down_map, up_map, before):
    _, third, width = codes.shape
    return pl.pallas_call(
        leave_kernel,
        in_specs=in_hbm(4) + [pl.BlockSpec(memory_space=pl.ANY)],
        out_specs=in_hbm(1) + [pl.BlockSpec(memory_space=pltpu.VMEM)],
        out_shape=[
            jax.ShapeDtypeStruct((3 * third, width), bf16),
            jax.ShapeDtypeStruct((8, LANES), f32),
        ],
        scratch_shapes=[
            pltpu.VMEM((third, width), jnp.int32),
            pltpu.VMEM(scale.shape[1:], bf16),
            pltpu.VMEM((RANK, 3 * third), bf16),
            pltpu.VMEM((RANK, width), bf16),
            pltpu.VMEM((3 * third, width), bf16),
            pltpu.SemaphoreType.DMA((3,)),
            pltpu.SemaphoreType.DMA((width // BLOCK,)),
            pltpu.SemaphoreType.DMA((width // BLOCK,)),
        ],
        compiler_params=params(58),
        cost_estimate=pl.CostEstimate(flops=2 * 10**9, bytes_accessed=15 * 10**6, transcendentals=0),
    )(codes, scale, down_map[0].T, up_map, before)


def pick_rows(own, tables, rows, slots):
    cap = rows // 2
    total = rows * len(tables)
    lane = lax.broadcasted_iota(jnp.int32, (rows, LANES), 1)
    columns = []
    for shift in (0, LANES // 2):
        parts = [
            jnp.sum(jnp.where(lane == own + shift, t, 0.0), axis=-1, keepdims=True) for t in tables
        ]
        column = jnp.concatenate(parts, axis=0)
        columns.append(jnp.broadcast_to(column, (total, slots)))
    high, low = columns
    hit = (high != 0.0).astype(f32).astype(bf16)
    high, low = high.astype(bf16), low.astype(bf16)
    row = lax.broadcasted_iota(jnp.int32, (total, total), 0)
    column = lax.broadcasted_iota(jnp.int32, (total, total), 1)
    before = ((row // rows == column // rows) & (row < column)).astype(f32).astype(bf16)
    first = (((0,), (0,)), ((), ()))
    rank_of = lax.dot_general(hit, before, first, preferred_element_type=f32)
    hit_of = lax.dot_general(hit, unit(total), first, preferred_element_type=f32)
    slot = lax.broadcasted_iota(jnp.int32, (slots, total), 0)
    place = lax.broadcasted_iota(jnp.int32, (slots, total), 1)
    taken = (slot // cap == place // rows) & (rank_of == (slot % cap).astype(f32)) & (hit_of > 0.5)
    gather = taken.astype(f32).astype(bf16)
    weight = jnp.dot(gather, high, preferred_element_type=f32)
    weight = weight + jnp.dot(gather, low, preferred_element_type=f32)
    rank = lax.dot_general(before, hit, first, preferred_element_type=f32)
    slot = lax.broadcasted_iota(jnp.int32, (total, slots), 1)
    place = lax.broadcasted_iota(jnp.int32, (total, slots), 0)
    taken = (slot // cap == place // rows) & (rank == (slot % cap).astype(f32)) & (hit.astype(f32) > 0.5)
    return gather, taken.astype(f32).astype(bf16), weight


def expert_kernel(count, pieces, own, *refs):
    blocks, refs = refs[:count], refs[count:]
    enters, leave, _, refs = refs[:pieces], refs[pieces], refs[pieces + 1], refs[pieces + 2 :]
    outs, refs = refs[:count], refs[count:]
    picked, spread, weight, active, enter_of, leave_of, enter_sem, leave_sem = refs
    rows = blocks[0].shape[0]
    width = picked.shape[1]
    sets, _, slots = spread.shape
    _, tiles, depth, _ = enter_of.shape
    each = count // sets
    wide = 4 * LANES
    steps = width // wide

    def enter_move(p, tile):
        return pltpu.make_async_copy(enters[p].at[tile], enter_of.at[p, tile], enter_sem.at[p, tile])

    def leave_move(n):
        lanes = pl.ds(pl.multiple_of(n * wide, wide), wide)
        return pltpu.make_async_copy(leave.at[:, lanes], leave_of.at[n], leave_sem.at[n])

    for tile in range(tiles):
        for p in range(pieces):
            enter_move(p, tile).start()
    for n in range(steps):
        leave_move(n).start()
    for g in range(sets):
        members = blocks[g * each : (g + 1) * each]
        tables = [member[:, width:].astype(f32) for member in members]
        gather, scatter, factor = pick_rows(own[0], tables, rows, slots)
        here = pl.ds(g * slots, slots)
        spread[g] = scatter
        weight[here, :] = factor
        for n in range(steps):
            lanes = pl.ds(n * wide, wide)
            source = jnp.concatenate([member[:, lanes] for member in members], axis=0)
            picked[here, lanes] = jnp.dot(gather, source, preferred_element_type=f32).astype(bf16)

    @pl.loop(0, tiles)
    def _(tile):
        joined = 0.0
        for p in range(pieces):
            enter_move(p, tile).wait()
            part = picked[:, pl.ds(p * depth, depth)]
            joined = joined + jnp.dot(part, enter_of[p, tile], preferred_element_type=f32)
        gate = joined[:, :LANES]
        value = gate / (1.0 + jnp.exp(-gate)) * joined[:, LANES:]
        active[tile] = value.astype(bf16)

    @pl.loop(0, steps)
    def _(n):
        leave_move(n).wait()
        lanes = pl.ds(pl.multiple_of(n * wide, wide), wide)
        entry = jnp.concatenate([active[t] for t in range(tiles)], axis=1)
        factor = jnp.concatenate([weight[...]] * (wide // slots), axis=1)
        result = jnp.dot(entry, leave_of[n], preferred_element_type=f32)
        result = (result * factor).astype(bf16)
        for g in range(sets):
            own_rows = result[g * slots : (g + 1) * slots]
            full = jnp.dot(spread[g], own_rows, preferred_element_type=f32).astype(bf16)
            for b in range(each):
                outs[g * each + b][:, lanes] = full[b * rows : (b + 1) * rows]


def expert(own, blocks, enters, leave, before):
    count = len(blocks)
    pieces = len(enters)
    rows, padded = blocks[0].shape
    width = padded - LANES
    tiles, depth, columns = enters[0].shape
    each = LANES // (rows // 2)
    sets = count // each
    steps = width // (4 * LANES)
    vmem = pl.BlockSpec(memory_space=pltpu.VMEM)
    return pl.pallas_call(
        functools.partial(expert_kernel, count, pieces),
        in_specs=[pl.BlockSpec(memory_space=pltpu.SMEM)]
        + [vmem] * count
        + in_hbm(pieces + 1)
        + [pl.BlockSpec(memory_space=pl.ANY)],
        out_specs=[vmem] * count,
        out_shape=[jax.ShapeDtypeStruct((rows, width), bf16)] * count,
        scratch_shapes=[
            pltpu.VMEM((sets * LANES, width), bf16),
            pltpu.VMEM((sets, each * rows, LANES), bf16),
            pltpu.VMEM((sets * LANES, LANES), f32),
            pltpu.VMEM((tiles, sets * LANES, LANES), bf16),
            pltpu.VMEM((pieces, tiles, depth, columns), bf16),
            pltpu.VMEM((steps, leave.shape[0], 4 * LANES), bf16),
            pltpu.SemaphoreType.DMA((pieces, tiles)),
            pltpu.SemaphoreType.DMA((steps,)),
        ],
        compiler_params=params(50),
        cost_estimate=pl.CostEstimate(flops=10**10, bytes_accessed=28 * 10**6, transcendentals=0),
    )(own, *blocks, *enters, leave, before)


def attend_kernel(lengths, queries, fresh, cache, out):
    rows = queries.shape[0]
    first = pl.program_id(0) * rows
    scaling = 1.0 / math.sqrt(HEAD)
    positions = cache.shape[2]
    lower = lax.broadcasted_iota(jnp.int32, (HEADS, HEAD), 0) < HEADS // KV_HEADS
    place = lax.broadcasted_iota(jnp.int32, (HEADS, positions), 1)
    own_half = lambda both: jnp.where(lower, both[:, :HEAD], both[:, HEAD:])
    old, new = [], []
    for t in range(rows):
        query = queries[t]
        zero = jnp.zeros_like(query)
        both = jnp.concatenate([jnp.where(lower, query, zero), jnp.where(lower, zero, query)], axis=1)
        score = lax.dot_general(
            both, cache[t, 0], (((1,), (1,)), ((), ())), preferred_element_type=f32
        )
        old.append(jnp.where(place < lengths[first + t], score * scaling, -jnp.inf))
        key = own_half(fresh[t, 0:1, :].astype(f32))
        new.append(jnp.sum(query.astype(f32) * key, axis=-1, keepdims=True) * scaling)
    old, new = jnp.concatenate(old, axis=0), jnp.concatenate(new, axis=0)
    highest = jnp.maximum(jnp.max(old, axis=-1, keepdims=True), new)
    old = jnp.exp(old - highest)
    new = jnp.exp(new - highest)
    inverse = 1.0 / (jnp.sum(old, axis=-1, keepdims=True) + new)
    old = (old * inverse).astype(bf16)
    new = (new * inverse).astype(bf16).astype(f32)
    for t in range(rows):
        heads = slice(t * HEADS, (t + 1) * HEADS)
        blended = own_half(jnp.dot(old[heads], cache[t, 1], preferred_element_type=f32))
        out[t] = (blended + new[heads] * own_half(fresh[t, 1:2, :].astype(f32))).astype(bf16)


def attend(queries, fresh_key_value, key_value_cache, lengths, block=8):
    rows = queries.shape[0]
    positions, width = key_value_cache.shape[2:]
    context = pl.pallas_call(
        attend_kernel,
        grid_spec=pltpu.PrefetchScalarGridSpec(
            num_scalar_prefetch=1,
            grid=(rows // block,),
            in_specs=[
                pl.BlockSpec((block, HEADS, HEAD), lambda i, _: (i, 0, 0)),
                pl.BlockSpec((block, 2, width), lambda i, _: (i, 0, 0)),
                pl.BlockSpec((block, 2, positions, width), lambda i, _: (i, 0, 0, 0)),
            ],
            out_specs=pl.BlockSpec((block, HEADS, HEAD), lambda i, _: (i, 0, 0)),
        ),
        out_shape=jax.ShapeDtypeStruct((rows, HEADS, HEAD), bf16),
        compiler_params=params(16),
        cost_estimate=pl.CostEstimate(flops=5 * 10**8, bytes_accessed=20 * 10**6, transcendentals=0),
    )(lengths, queries.reshape(rows, HEADS, HEAD), fresh_key_value, key_value_cache)
    return context.reshape(rows, HEADS * HEAD)


def swap(value, bit):
    count = lax.axis_size("ep")
    return lax.ppermute(value, "ep", [(i, i ^ bit) for i in range(count)])


def add(terms):
    return sum(term.astype(f32) for term in terms[1:]) + terms[0].astype(f32)


def shards(
    queries,
    fresh_key_value,
    key_value_cache,
    lengths,
    hidden,
    expert_norm_gain,
    routes,
    router_scores,
    gate_up_quant_codes,
    gate_up_code_scale,
    down_quant_codes,
    down_code_scale,
    adapter_input_down,
    adapter_input_up,
    adapter_output_down,
    adapter_output_up,
):
    count = lax.axis_size("ep")
    bits = [1 << b for b in range(count.bit_length() - 1)]
    blocks = {0: norm_rows(hidden, expert_norm_gain, routes, router_scores)}
    enter = [
        lambda before, p=p: enter_weights(
            p, 2, gate_up_quant_codes, gate_up_code_scale, adapter_input_down, adapter_input_up, before
        )
        for p in range(2)
    ]
    leave = lambda before: leave_weights(
        down_quant_codes, down_code_scale, adapter_output_down, adapter_output_up, before
    )
    stage = lambda r: sum(1 for bit in bits[1:] if r & bit)
    low_bit = lambda r: r & -r
    even = [r for r in range(count) if r and r % 2 == 0]
    weights = []
    done = jnp.zeros((8, LANES), f32)
    for now in range(max(stage(r) for r in even) + 1):
        for r in sorted(even, key=low_bit, reverse=True):
            if stage(r ^ low_bit(r)) == now:
                blocks[r] = swap(blocks[r ^ low_bit(r)], low_bit(r))
        for r in [0] + even:
            if stage(r) == now:
                blocks[r | 1] = swap(blocks[r], 1)
        arriving = [r for r in blocks if r % 2 == 0 and stage(r) == now + 1]
        if now < 3:
            made, done = (enter + [leave])[now](done)
            weights.append(made)
            *held, done = lax.optimization_barrier((*[blocks[r] for r in arriving], done))
            blocks.update(zip(arriving, held))
    own = lax.axis_index("ep").astype(jnp.int32).reshape(1)
    produced = expert(own, [blocks[r] for r in range(count)], weights[:2], weights[2], done)
    after = lambda earlier, later: list(lax.optimization_barrier((earlier, *later)))
    sums = {r: [produced[r]] for r in range(0, count, 2)}
    other = {r: produced[r | 1] for r in sums}
    first = max(sums)
    sums[first].append(swap(other.pop(first), 1))
    sent = add(sums.pop(first)).astype(bf16)
    sent, queries, *rest = after(sent, [queries] + [other[r] for r in other])
    for r, rows in zip(other, rest):
        sums[r].append(swap(rows, 1))
    near = bits[1]
    arrived = swap(sent, near)
    context = attend(queries, fresh_key_value, key_value_cache, lengths)
    arrived, context = after(arrived, [context])
    sums[first ^ near].append(arrived)
    for r in sorted(sums, reverse=True)[:-1]:
        bit = low_bit(r)
        sent = add(sums.pop(r)).astype(bf16)
        if bit == near:
            arrived, sent = after(arrived, [sent])
        received = swap(sent, bit)
        if bit == near:
            arrived = received
        sums[r ^ bit].append(received)
    return (context, add(sums[0]).astype(bf16))


def solution(mesh):
    return jax.shard_map(
        shards,
        mesh=mesh,
        in_specs=(
            P(("grp", "ep"), None),
            P(("grp", "ep"), None, None),
            P(("grp", "ep"), None, None, None),
            P(("grp", "ep")),
            P(("grp", "ep"), None),
            P(),
            P(("grp", "ep"), None),
            P(("grp", "ep"), None),
            P("ep", None, None),
            P("ep", None, None),
            P("ep", None, None),
            P("ep", None, None),
            P("ep", None, None),
            P("ep", None, None, None),
            P("ep", None, None),
            P("ep", None, None),
        ),
        out_specs=(P(("grp", "ep"), None), P(("grp", "ep"), None)),
        check_vma=False,
    )
```

```python
import functools
import math

import jax
import jax.numpy as jnp
from jax import lax
from jax.experimental import pallas as pl
from jax.experimental.pallas import tpu as pltpu
from jax.sharding import PartitionSpec as P

HEADS = 32
KV_HEADS = 2
HEAD = 128
RANK = 16
LANES = 128
GROUP = 64
FLYING = 3
AHEAD = 2
BLOCK = 512
code_levels = (
    -1.0,
    -0.6961928009986877,
    -0.5250730514526367,
    -0.39491748809814453,
    -0.28444138169288635,
    -0.18477343022823334,
    -0.09105003625154495,
    0.0,
    0.07958029955625534,
    0.16093020141124725,
    0.24611230194568634,
    0.33791524171829224,
    0.44070982933044434,
    0.5626170039176941,
    0.7229568362236023,
    1.0,
)
adapter_scale = 2.0
norm_epsilon = 1e-06
f32 = jnp.float32
bf16 = jnp.bfloat16


def params(mib):
    return pltpu.CompilerParams(vmem_limit_bytes=mib * 2**20)


def whole(shape):
    return pl.BlockSpec(shape, lambda *_: (0,) * len(shape))


def norm_kernel(hidden, gain, routes, scores, out):
    rows, width = hidden.shape
    wide = hidden[...].astype(f32)
    spread = jnp.mean(wide * wide, axis=-1, keepdims=True)
    normed = wide * lax.rsqrt(spread + norm_epsilon) * gain[...].astype(f32).reshape(1, width)
    out[:, :width] = normed.astype(bf16)
    logits = scores[...]
    parts = jnp.exp(logits - jnp.max(logits, axis=0, keepdims=True))
    shares = parts / jnp.sum(parts, axis=0, keepdims=True)
    place = lax.broadcasted_iota(jnp.int32, (LANES, rows), 0)
    named = place & (LANES // 2 - 1)
    table = jnp.zeros((LANES, rows), f32)
    for k in range(routes.shape[0]):
        table = table + jnp.where(routes[k : k + 1, :] == named, shares[k : k + 1, :], 0.0)
    high = table.astype(bf16).astype(f32)
    both = jnp.where(place < LANES // 2, high, table - high).astype(bf16)
    out[:, width:] = lax.dot_general(
        unit(rows), both, (((1,), (1,)), ((), ())), preferred_element_type=f32
    ).astype(bf16)


def unit(size):
    row = lax.broadcasted_iota(jnp.int32, (size, size), 0)
    return (row == lax.broadcasted_iota(jnp.int32, (size, size), 1)).astype(f32).astype(bf16)


def norm_rows(hidden, gain, routes, scores):
    rows, width = hidden.shape
    top = routes.shape[1]
    return pl.pallas_call(
        norm_kernel,
        grid=(1,),
        in_specs=[whole((rows, width)), whole((width,)), whole((top, rows)), whole((top, rows))],
        out_specs=whole((rows, width + LANES)),
        out_shape=jax.ShapeDtypeStruct((rows, width + LANES), bf16),
        compiler_params=params(56),
    )(hidden, gain, routes.T, scores.T)


def level_tables():
    sub = lax.broadcasted_iota(jnp.int32, (8, LANES), 0)
    low = jnp.zeros((8, LANES), f32)
    high = low
    for i in range(8):
        low = jnp.where(sub == i, code_levels[i], low)
        high = jnp.where(sub == i, code_levels[i + 8], high)
    return low, high


def decode(tables, words, nibble):
    pieces = []
    for q in range(words.shape[0] // 8):
        word = words[8 * q : 8 * q + 8]
        entry = (word >> (4 * nibble)) & 7
        upper = (word & (8 << (4 * nibble))) != 0
        low = jnp.take_along_axis(tables[0], entry, axis=0, mode="promise_in_bounds")
        high = jnp.take_along_axis(tables[1], entry, axis=0, mode="promise_in_bounds")
        pieces.append(jnp.where(upper, high, low))
    return jnp.concatenate(pieces, axis=0)


def copy(source, target, sem):
    move = pltpu.make_async_copy(source, target, sem)
    move.start()
    return move


def enter_kernel(
    part, rows, codes, scale, down_map, up_map, before, held, out, made,
    words_of, scale_of, factors, down_of, up_of, spread, weights, small_sem, in_sem, out_sem,
):
    tiles = out.shape[0]
    third = codes.shape[2]
    half = tiles * LANES
    first = part * rows
    blocks = rows // BLOCK
    arriving = [
        copy(scale.at[0, pl.ds(first // GROUP, rows // GROUP)], scale_of, small_sem.at[0]),
        copy(down_map.at[:, pl.ds(first, rows)], down_of, small_sem.at[1]),
        copy(up_map.at[0], up_of, small_sem.at[2]),
    ]

    def arriving_words(k):
        here = pl.multiple_of(k * BLOCK, BLOCK)
        return pltpu.make_async_copy(
            codes.at[0, pl.ds(first + here, BLOCK)], words_of.at[pl.ds(here, BLOCK)], in_sem.at[k]
        )

    for k in range(AHEAD):
        arriving_words(k).start()
    made[...] = jnp.zeros_like(made)
    tables = level_tables()
    spread[...] = jnp.zeros_like(spread)
    for move in arriving:
        move.wait()
    for tile in range(tiles):
        for side in range(2):
            piece = up_of[side, :, tile * LANES : (tile + 1) * LANES].astype(f32) * adapter_scale
            spread[tile, side * RANK : (side + 1) * RANK, side * LANES : (side + 1) * LANES] = piece.astype(bf16)
    factors[...] = scale_of[...].astype(f32)
    scales = BLOCK // GROUP

    def leaving(k):
        here = pl.ds(pl.multiple_of(k * BLOCK, BLOCK), BLOCK)
        there = pl.ds(pl.multiple_of(first + k * BLOCK, BLOCK), BLOCK)
        return pltpu.make_async_copy(weights.at[:, here], out.at[:, there], out_sem.at[k])

    @pl.loop(0, blocks)
    def _(k):
        arriving_words(k).wait()

        @pl.when(k + AHEAD < blocks)
        def _():
            arriving_words(k + AHEAD).start()

        here = pl.multiple_of(k * BLOCK, BLOCK)
        for tile in range(tiles):
            adapter = lax.dot_general(
                down_of[:, pl.ds(here, BLOCK)],
                spread[tile],
                (((0,), (0,)), ((), ())),
                preferred_element_type=f32,
            )
            for side in range(2):
                column = side * half + tile * LANES
                nibble, offset = divmod(column, third)
                factor = factors[pl.ds(pl.multiple_of(k * scales, scales), scales), pl.ds(column, LANES)]
                for g in range(scales):
                    packed = words_of[pl.ds(here + g * GROUP, GROUP), pl.ds(offset, LANES)]
                    value = decode(tables, packed, nibble) * factor[g : g + 1]
                    value = value + adapter[g * GROUP : (g + 1) * GROUP, side * LANES : (side + 1) * LANES]
                    weights[tile, pl.ds(here + g * GROUP, GROUP), pl.ds(side * LANES, LANES)] = value.astype(bf16)
        leaving(k).start()

    @pl.loop(0, blocks)
    def _(k):
        leaving(k).wait()


def in_hbm(count):
    return [pl.BlockSpec(memory_space=pltpu.HBM)] * count


def enter_weights(part, parts, codes, scale, down_map, up_map, before, held):
    _, width, third = codes.shape
    tiles = 3 * third // 2 // LANES
    rows = width // parts
    return pl.pallas_call(
        functools.partial(enter_kernel, part, rows),
        in_specs=in_hbm(4) + [pl.BlockSpec(memory_space=pl.ANY)] * 2,
        out_specs=in_hbm(1) + [pl.BlockSpec(memory_space=pltpu.VMEM)],
        input_output_aliases={5: 0} if part else {},
        out_shape=[
            jax.ShapeDtypeStruct((tiles, width, 2 * LANES), bf16),
            jax.ShapeDtypeStruct((8, LANES), f32),
        ],
        scratch_shapes=[
            pltpu.VMEM((rows, third), jnp.int32),
            pltpu.VMEM((rows // GROUP, 3 * third), bf16),
            pltpu.VMEM((rows // GROUP, 3 * third), f32),
            pltpu.VMEM((2 * RANK, rows), bf16),
            pltpu.VMEM(up_map.shape[1:], bf16),
            pltpu.VMEM((tiles, 2 * RANK, 2 * LANES), bf16),
            pltpu.VMEM((tiles, rows, 2 * LANES), bf16),
            pltpu.SemaphoreType.DMA((3,)),
            pltpu.SemaphoreType.DMA((rows // BLOCK,)),
            pltpu.SemaphoreType.DMA((rows // BLOCK,)),
        ],
        compiler_params=params(56),
        cost_estimate=pl.CostEstimate(flops=4 * 10**9, bytes_accessed=20 * 10**6, transcendentals=0),
    )(codes, scale, down_map[0].T, up_map, before, held)


class Leave:
    def __init__(self, codes, scale, down_map, up_map, scratch):
        self.words, self.scale, self.down, self.up, self.weights, self.sems = scratch
        self.pairs = [
            (codes.at[0], self.words),
            (scale.at[0], self.scale),
            (down_map, self.down),
            (up_map.at[0], self.up),
        ]

    @staticmethod
    def scratch(codes, scale, up_map):
        _, third, width = codes.shape
        return [
            pltpu.VMEM((third, width), jnp.int32),
            pltpu.VMEM(scale.shape[1:], bf16),
            pltpu.VMEM((RANK, 3 * third), bf16),
            pltpu.VMEM(up_map.shape[1:], bf16),
            pltpu.VMEM((3 * third, width), bf16),
            pltpu.SemaphoreType.DMA((4,)),
        ]

    def start(self):
        self.moves = [copy(a, b, self.sems.at[i]) for i, (a, b) in enumerate(self.pairs)]

    def ready(self):
        for move in self.moves:
            move.wait()

    def decode(self, tables, strip, strips):
        rows = self.words.shape[0]
        first = strip * LANES if isinstance(strip, int) else pl.multiple_of(strip * LANES, LANES)
        adapter = lax.dot_general(
            self.down[...],
            self.up[:, pl.ds(first, strips * LANES)],
            (((0,), (0,)), ((), ())),
            preferred_element_type=f32,
        ) * adapter_scale
        for j in range(strips):
            here = pl.ds(first + j * LANES, LANES)
            for nibble in range(3):
                for g in range(rows // GROUP):
                    row = nibble * rows + g * GROUP
                    packed = self.words[pl.ds(g * GROUP, GROUP), here]
                    factor = self.scale[pl.ds(row // GROUP, 1), here].astype(f32)
                    value = decode(tables, packed, nibble) * factor
                    value = value + adapter[row : row + GROUP, j * LANES : (j + 1) * LANES]
                    self.weights[pl.ds(row, GROUP), here] = value.astype(bf16)


def pick_rows(own, tables, rows, slots):
    cap = rows // 2
    total = rows * len(tables)
    lane = lax.broadcasted_iota(jnp.int32, (rows, LANES), 1)
    columns = []
    for shift in (0, LANES // 2):
        parts = [
            jnp.sum(jnp.where(lane == own + shift, t, 0.0), axis=-1, keepdims=True) for t in tables
        ]
        column = jnp.concatenate(parts, axis=0)
        columns.append(jnp.broadcast_to(column, (total, slots)))
    high, low = columns
    hit = (high != 0.0).astype(f32).astype(bf16)
    high, low = high.astype(bf16), low.astype(bf16)
    row = lax.broadcasted_iota(jnp.int32, (total, total), 0)
    column = lax.broadcasted_iota(jnp.int32, (total, total), 1)
    before = ((row // rows == column // rows) & (row < column)).astype(f32).astype(bf16)
    first = (((0,), (0,)), ((), ()))
    rank_of = lax.dot_general(hit, before, first, preferred_element_type=f32)
    hit_of = lax.dot_general(hit, unit(total), first, preferred_element_type=f32)
    slot = lax.broadcasted_iota(jnp.int32, (slots, total), 0)
    place = lax.broadcasted_iota(jnp.int32, (slots, total), 1)
    taken = (slot // cap == place // rows) & (rank_of == (slot % cap).astype(f32)) & (hit_of > 0.5)
    gather = taken.astype(f32).astype(bf16)
    weight = jnp.dot(gather, high, preferred_element_type=f32)
    weight = weight + jnp.dot(gather, low, preferred_element_type=f32)
    rank = lax.dot_general(before, hit, first, preferred_element_type=f32)
    slot = lax.broadcasted_iota(jnp.int32, (total, slots), 1)
    place = lax.broadcasted_iota(jnp.int32, (total, slots), 0)
    taken = (slot // cap == place // rows) & (rank == (slot % cap).astype(f32)) & (hit.astype(f32) > 0.5)
    return gather, taken.astype(f32).astype(bf16), weight


def expert_kernel(count, own, *refs):
    blocks, refs = refs[:count], refs[count:]
    enter, codes, scale, down_map, up_map, _ = refs[:6]
    outs, refs = refs[6 : count + 6], refs[count + 6 :]
    picked, spread, weight, active, enter_of, enter_sem = refs[:6]
    leave = Leave(codes, scale, down_map, up_map, refs[6:])
    leave.start()
    rows = blocks[0].shape[0]
    width = picked.shape[1]
    sets, span, slots = spread.shape
    tiles = enter_of.shape[0]
    each = count // sets
    wide = 8 * LANES

    def arriving(tile):
        return pltpu.make_async_copy(enter.at[tile], enter_of.at[tile], enter_sem.at[tile])

    for tile in range(FLYING):
        arriving(tile).start()
    for g in range(sets):
        members = blocks[g * each : (g + 1) * each]
        tables = [member[:, width:].astype(f32) for member in members]
        gather, scatter, factor = pick_rows(own[0], tables, rows, slots)
        here = pl.ds(g * slots, slots)
        spread[g] = scatter
        weight[here, :] = factor
        for n in range(width // wide):
            lanes = pl.ds(n * wide, wide)
            source = jnp.concatenate([member[:, lanes] for member in members], axis=0)
            picked[here, lanes] = jnp.dot(gather, source, preferred_element_type=f32).astype(bf16)
    levels = level_tables()
    leave.ready()
    strips = width // LANES
    per_tile = strips // tiles

    @pl.loop(0, tiles)
    def _(tile):
        arriving(tile).wait()

        @pl.when(tile + FLYING < tiles)
        def _():
            arriving(tile + FLYING).start()

        joined = jnp.dot(picked[...], enter_of[tile], preferred_element_type=f32)
        leave.decode(levels, tile * per_tile, per_tile)
        gate = joined[:, :LANES]
        value = gate / (1.0 + jnp.exp(-gate)) * joined[:, LANES:]
        active[tile] = value.astype(bf16)

    if tiles * per_tile < strips:
        leave.decode(levels, tiles * per_tile, strips - tiles * per_tile)

    @pl.loop(0, width // wide)
    def _(n):
        lanes = pl.ds(pl.multiple_of(n * wide, wide), wide)
        entry = jnp.concatenate([active[t] for t in range(tiles)], axis=1)
        factor = jnp.concatenate([weight[...]] * (wide // slots), axis=1)
        result = jnp.dot(entry, leave.weights[:, lanes], preferred_element_type=f32)
        result = (result * factor).astype(bf16)
        for g in range(sets):
            own_rows = result[g * slots : (g + 1) * slots]
            full = jnp.dot(spread[g], own_rows, preferred_element_type=f32).astype(bf16)
            for b in range(each):
                outs[g * each + b][:, lanes] = full[b * rows : (b + 1) * rows]


def expert(own, blocks, enter, codes, scale, down_map, up_map, before):
    count = len(blocks)
    tiles = enter.shape[0]
    rows, padded = blocks[0].shape
    width = padded - LANES
    each = LANES // (rows // 2)
    sets = count // each
    vmem = pl.BlockSpec(memory_space=pltpu.VMEM)
    return pl.pallas_call(
        functools.partial(expert_kernel, count),
        in_specs=[pl.BlockSpec(memory_space=pltpu.SMEM)]
        + [vmem] * count
        + in_hbm(5)
        + [pl.BlockSpec(memory_space=pl.ANY)],
        out_specs=[vmem] * count,
        out_shape=[jax.ShapeDtypeStruct((rows, width), bf16)] * count,
        scratch_shapes=[
            pltpu.VMEM((sets * LANES, width), bf16),
            pltpu.VMEM((sets, each * rows, LANES), bf16),
            pltpu.VMEM((sets * LANES, LANES), f32),
            pltpu.VMEM((tiles, sets * LANES, LANES), bf16),
            pltpu.VMEM(enter.shape, bf16),
            pltpu.SemaphoreType.DMA((tiles,)),
        ]
        + Leave.scratch(codes, scale, up_map),
        compiler_params=params(46),
        cost_estimate=pl.CostEstimate(flops=8 * 10**9, bytes_accessed=22 * 10**6, transcendentals=0),
    )(own, *blocks, enter, codes, scale, down_map[0].T, up_map, before)


def attend_kernel(
    lengths, queries, fresh, cache, _, out, queries_of, fresh_of, cache_of, small_sem, cache_sem, *, first, block
):
    rows = out.shape[0]
    mine = pl.ds(first, rows)
    scaling = 1.0 / math.sqrt(HEAD)
    positions = cache.shape[2]
    small = [copy(queries.at[mine], queries_of, small_sem.at[0]), copy(fresh.at[mine], fresh_of, small_sem.at[1])]

    def arriving(k):
        there = pl.ds(first + k * block, block)
        return pltpu.make_async_copy(cache.at[there], cache_of.at[pl.ds(k * block, block)], cache_sem.at[k])

    for k in range(rows // block):
        arriving(k).start()
    lower = lax.broadcasted_iota(jnp.int32, (HEADS, HEAD), 0) < HEADS // KV_HEADS
    place = lax.broadcasted_iota(jnp.int32, (HEADS, positions), 1)
    own_half = lambda both: jnp.where(lower, both[:, :HEAD], both[:, HEAD:])
    for move in small:
        move.wait()

    @pl.loop(0, rows // block)
    def _(k):
        arriving(k).wait()
        old, new = [], []
        for t in range(block):
            row = k * block + t
            query = queries_of[row]
            zero = jnp.zeros_like(query)
            both = jnp.concatenate([jnp.where(lower, query, zero), jnp.where(lower, zero, query)], axis=1)
            score = lax.dot_general(
                both, cache_of[row, 0], (((1,), (1,)), ((), ())), preferred_element_type=f32
            )
            old.append(jnp.where(place < lengths[first + row], score * scaling, -jnp.inf))
            key = own_half(fresh_of[row, 0:1, :].astype(f32))
            new.append(jnp.sum(query.astype(f32) * key, axis=-1, keepdims=True) * scaling)
        old, new = jnp.concatenate(old, axis=0), jnp.concatenate(new, axis=0)
        highest = jnp.maximum(jnp.max(old, axis=-1, keepdims=True), new)
        old = jnp.exp(old - highest)
        new = jnp.exp(new - highest)
        inverse = 1.0 / (jnp.sum(old, axis=-1, keepdims=True) + new)
        old = (old * inverse).astype(bf16)
        new = (new * inverse).astype(bf16).astype(f32)
        for t in range(block):
            row = k * block + t
            heads = slice(t * HEADS, (t + 1) * HEADS)
            blended = own_half(jnp.dot(old[heads], cache_of[row, 1], preferred_element_type=f32))
            out[row] = (blended + new[heads] * own_half(fresh_of[row, 1:2, :].astype(f32))).astype(bf16)


def attend(queries, fresh_key_value, key_value_cache, lengths, before, part, parts, block=8):
    rows = queries.shape[0] // parts
    return pl.pallas_call(
        functools.partial(attend_kernel, first=part * rows, block=block),
        in_specs=[pl.BlockSpec(memory_space=pltpu.SMEM)] + in_hbm(3) + [pl.BlockSpec(memory_space=pl.ANY)],
        out_specs=pl.BlockSpec(memory_space=pltpu.VMEM),
        out_shape=jax.ShapeDtypeStruct((rows, HEADS, HEAD), bf16),
        scratch_shapes=[
            pltpu.VMEM((rows, HEADS, HEAD), bf16),
            pltpu.VMEM((rows, *fresh_key_value.shape[1:]), bf16),
            pltpu.VMEM((rows, *key_value_cache.shape[1:]), bf16),
            pltpu.SemaphoreType.DMA((2,)),
            pltpu.SemaphoreType.DMA((rows // block,)),
        ],
        compiler_params=params(49),
        cost_estimate=pl.CostEstimate(flops=5 * 10**8, bytes_accessed=20 * 10**6, transcendentals=0),
    )(lengths, queries, fresh_key_value, key_value_cache, before)


def swap(value, bit):
    count = lax.axis_size("ep")
    return lax.ppermute(value, "ep", [(i, i ^ bit) for i in range(count)])


def add(terms):
    return sum(term.astype(f32) for term in terms[1:]) + terms[0].astype(f32)


def shards(
    queries,
    fresh_key_value,
    key_value_cache,
    lengths,
    hidden,
    expert_norm_gain,
    routes,
    router_scores,
    gate_up_quant_codes,
    gate_up_code_scale,
    down_quant_codes,
    down_code_scale,
    adapter_input_down,
    adapter_input_up,
    adapter_output_down,
    adapter_output_up,
):
    count = lax.axis_size("ep")
    bits = [1 << b for b in range(count.bit_length() - 1)]
    rows = hidden.shape[0]
    blocks = {0: norm_rows(hidden, expert_norm_gain, routes, router_scores)}
    leave_args = (down_quant_codes, down_code_scale, adapter_output_down, adapter_output_up)

    heads = queries.reshape(rows, HEADS, HEAD)
    attention = functools.partial(attend, heads, fresh_key_value, key_value_cache, lengths, parts=2)

    def make_enter(part, before, held):
        return enter_weights(
            part, 2, gate_up_quant_codes, gate_up_code_scale, adapter_input_down, adapter_input_up, before, held
        )

    stage = lambda r: sum(1 for bit in bits[1:] if r & bit)
    low_bit = lambda r: r & -r
    even = [r for r in range(count) if r and r % 2 == 0]
    done = blocks[0]
    for now in range(max(stage(r) for r in even) + 1):
        for r in sorted(even, key=low_bit, reverse=True):
            if stage(r ^ low_bit(r)) == now:
                blocks[r] = swap(blocks[r ^ low_bit(r)], low_bit(r))
        for r in [0] + even:
            if stage(r) == now:
                blocks[r | 1] = swap(blocks[r], 1)
        arriving = [r for r in blocks if r % 2 == 0 and stage(r) == now + 1]
        held = [blocks[r] for r in arriving]
        if now < 2:
            weights, done = make_enter(now, done, weights if now else done)
        elif now == 2:
            done = context = attention(done, 0)
        *held, done = lax.optimization_barrier((*held, done))
        if now == 2:
            context = done
        blocks.update(zip(arriving, held))
    own = lax.axis_index("ep").astype(jnp.int32).reshape(1)
    produced = expert(own, [blocks[r] for r in range(count)], weights, *leave_args, done)

    tie = lambda *values: list(lax.optimization_barrier(values))
    sums = {r: [produced[r]] for r in range(0, count, 2)}
    first = count - 2
    sent = add([sums.pop(first)[0], swap(produced[first + 1], 1)]).astype(bf16)
    sent, *others = tie(sent, *[produced[r + 1] for r in sums])
    arrived = swap(sent, bits[1])
    for r, value in zip(sums, others):
        sums[r].append(swap(value, 1))
    early = (first - 2, first - 4)
    before, *held = tie(sent, *[sums[r][1] for r in early])
    for r, value in zip(early, held):
        sums[r][1] = value
    later = attention(before, 1)
    arrived, later = tie(arrived, later)
    context = jnp.concatenate([context, later]).reshape(rows, HEADS * HEAD)
    sums[first ^ bits[1]].append(arrived)
    for r in range(first - 2, 0, -4):
        pair = tie(*[add(sums.pop(q)).astype(bf16) for q in (r, r - 2)])
        for q, value in zip((r, r - 2), pair):
            sums[q ^ low_bit(q)].append(swap(value, low_bit(q)))
    return (context, add(sums[0]).astype(bf16))


def solution(mesh):
    return jax.shard_map(
        shards,
        mesh=mesh,
        in_specs=(
            P(("grp", "ep"), None),
            P(("grp", "ep"), None, None),
            P(("grp", "ep"), None, None, None),
            P(("grp", "ep")),
            P(("grp", "ep"), None),
            P(),
            P(("grp", "ep"), None),
            P(("grp", "ep"), None),
            P("ep", None, None),
            P("ep", None, None),
            P("ep", None, None),
            P("ep", None, None),
            P("ep", None, None),
            P("ep", None, None, None),
            P("ep", None, None),
            P("ep", None, None),
        ),
        out_specs=(P(("grp", "ep"), None), P(("grp", "ep"), None)),
        check_vma=False,
    )
```

```python
import functools
import math

import jax
import jax.numpy as jnp
from jax import lax
from jax.experimental import pallas as pl
from jax.experimental.pallas import tpu as pltpu
from jax.sharding import PartitionSpec as P

HEADS = 32
KV_HEADS = 2
HEAD = 128
RANK = 16
LANES = 128
GROUP = 64
FLYING = 3
AHEAD = 2
BLOCK = 512
code_levels = (
    -1.0,
    -0.6961928009986877,
    -0.5250730514526367,
    -0.39491748809814453,
    -0.28444138169288635,
    -0.18477343022823334,
    -0.09105003625154495,
    0.0,
    0.07958029955625534,
    0.16093020141124725,
    0.24611230194568634,
    0.33791524171829224,
    0.44070982933044434,
    0.5626170039176941,
    0.7229568362236023,
    1.0,
)
adapter_scale = 2.0
norm_epsilon = 1e-06
f32 = jnp.float32
bf16 = jnp.bfloat16


def params(mib):
    return pltpu.CompilerParams(vmem_limit_bytes=mib * 2**20)


def whole(shape):
    return pl.BlockSpec(shape, lambda *_: (0,) * len(shape))


def norm_kernel(hidden, gain, routes, scores, out):
    rows, width = hidden.shape
    wide = hidden[...].astype(f32)
    spread = jnp.mean(wide * wide, axis=-1, keepdims=True)
    normed = wide * lax.rsqrt(spread + norm_epsilon) * gain[...].astype(f32).reshape(1, width)
    out[:, :width] = normed.astype(bf16)
    logits = scores[...]
    parts = jnp.exp(logits - jnp.max(logits, axis=0, keepdims=True))
    shares = parts / jnp.sum(parts, axis=0, keepdims=True)
    place = lax.broadcasted_iota(jnp.int32, (LANES, rows), 0)
    named = place & (LANES // 2 - 1)
    table = jnp.zeros((LANES, rows), f32)
    for k in range(routes.shape[0]):
        table = table + jnp.where(routes[k : k + 1, :] == named, shares[k : k + 1, :], 0.0)
    high = table.astype(bf16).astype(f32)
    both = jnp.where(place < LANES // 2, high, table - high).astype(bf16)
    out[:, width:] = lax.dot_general(
        unit(rows), both, (((1,), (1,)), ((), ())), preferred_element_type=f32
    ).astype(bf16)


def unit(size):
    row = lax.broadcasted_iota(jnp.int32, (size, size), 0)
    return (row == lax.broadcasted_iota(jnp.int32, (size, size), 1)).astype(f32).astype(bf16)


def norm_rows(hidden, gain, routes, scores):
    rows, width = hidden.shape
    top = routes.shape[1]
    return pl.pallas_call(
        norm_kernel,
        grid=(1,),
        in_specs=[whole((rows, width)), whole((width,)), whole((top, rows)), whole((top, rows))],
        out_specs=whole((rows, width + LANES)),
        out_shape=jax.ShapeDtypeStruct((rows, width + LANES), bf16),
        compiler_params=params(56),
    )(hidden, gain, routes.T, scores.T)


def level_tables():
    sub = lax.broadcasted_iota(jnp.int32, (8, LANES), 0)
    low = jnp.zeros((8, LANES), f32)
    high = low
    for i in range(8):
        low = jnp.where(sub == i, code_levels[i], low)
        high = jnp.where(sub == i, code_levels[i + 8], high)
    return low, high


def decode(tables, words, nibble):
    pieces = []
    for q in range(words.shape[0] // 8):
        word = words[8 * q : 8 * q + 8]
        entry = (word >> (4 * nibble)) & 7
        upper = (word & (8 << (4 * nibble))) != 0
        low = jnp.take_along_axis(tables[0], entry, axis=0, mode="promise_in_bounds")
        high = jnp.take_along_axis(tables[1], entry, axis=0, mode="promise_in_bounds")
        pieces.append(jnp.where(upper, high, low))
    return jnp.concatenate(pieces, axis=0)


def copy(source, target, sem):
    move = pltpu.make_async_copy(source, target, sem)
    move.start()
    return move


def enter_kernel(
    part, rows, codes, scale, down_map, up_map, before, held, out, made,
    words_of, scale_of, factors, down_of, up_of, spread, weights, small_sem, in_sem, out_sem,
):
    tiles = out.shape[0]
    third = codes.shape[2]
    half = tiles * LANES
    first = part * rows
    blocks = rows // BLOCK
    arriving = [
        copy(scale.at[0, pl.ds(first // GROUP, rows // GROUP)], scale_of, small_sem.at[0]),
        copy(down_map.at[:, pl.ds(first, rows)], down_of, small_sem.at[1]),
        copy(up_map.at[0], up_of, small_sem.at[2]),
    ]

    def arriving_words(k):
        here = pl.multiple_of(k * BLOCK, BLOCK)
        return pltpu.make_async_copy(
            codes.at[0, pl.ds(first + here, BLOCK)], words_of.at[pl.ds(here, BLOCK)], in_sem.at[k]
        )

    for k in range(AHEAD):
        arriving_words(k).start()
    made[...] = jnp.zeros_like(made)
    tables = level_tables()
    spread[...] = jnp.zeros_like(spread)
    for move in arriving:
        move.wait()
    for tile in range(tiles):
        for side in range(2):
            piece = up_of[side, :, tile * LANES : (tile + 1) * LANES].astype(f32) * adapter_scale
            spread[tile, side * RANK : (side + 1) * RANK, side * LANES : (side + 1) * LANES] = piece.astype(bf16)
    factors[...] = scale_of[...].astype(f32)
    scales = BLOCK // GROUP

    def leaving(k):
        here = pl.ds(pl.multiple_of(k * BLOCK, BLOCK), BLOCK)
        there = pl.ds(pl.multiple_of(first + k * BLOCK, BLOCK), BLOCK)
        return pltpu.make_async_copy(weights.at[:, here], out.at[:, there], out_sem.at[k])

    @pl.loop(0, blocks)
    def _(k):
        arriving_words(k).wait()

        @pl.when(k + AHEAD < blocks)
        def _():
            arriving_words(k + AHEAD).start()

        here = pl.multiple_of(k * BLOCK, BLOCK)
        for tile in range(tiles):
            adapter = lax.dot_general(
                down_of[:, pl.ds(here, BLOCK)],
                spread[tile],
                (((0,), (0,)), ((), ())),
                preferred_element_type=f32,
            )
            for side in range(2):
                column = side * half + tile * LANES
                nibble, offset = divmod(column, third)
                factor = factors[pl.ds(pl.multiple_of(k * scales, scales), scales), pl.ds(column, LANES)]
                for g in range(scales):
                    packed = words_of[pl.ds(here + g * GROUP, GROUP), pl.ds(offset, LANES)]
                    value = decode(tables, packed, nibble) * factor[g : g + 1]
                    value = value + adapter[g * GROUP : (g + 1) * GROUP, side * LANES : (side + 1) * LANES]
                    weights[tile, pl.ds(here + g * GROUP, GROUP), pl.ds(side * LANES, LANES)] = value.astype(bf16)
        leaving(k).start()

    @pl.loop(0, blocks)
    def _(k):
        leaving(k).wait()


def in_hbm(count):
    return [pl.BlockSpec(memory_space=pltpu.HBM)] * count


def enter_weights(part, parts, codes, scale, down_map, up_map, before, held):
    _, width, third = codes.shape
    tiles = 3 * third // 2 // LANES
    rows = width // parts
    return pl.pallas_call(
        functools.partial(enter_kernel, part, rows),
        in_specs=in_hbm(4) + [pl.BlockSpec(memory_space=pl.ANY)] * 2,
        out_specs=in_hbm(1) + [pl.BlockSpec(memory_space=pltpu.VMEM)],
        input_output_aliases={5: 0} if part else {},
        out_shape=[
            jax.ShapeDtypeStruct((tiles, width, 2 * LANES), bf16),
            jax.ShapeDtypeStruct((8, LANES), f32),
        ],
        scratch_shapes=[
            pltpu.VMEM((rows, third), jnp.int32),
            pltpu.VMEM((rows // GROUP, 3 * third), bf16),
            pltpu.VMEM((rows // GROUP, 3 * third), f32),
            pltpu.VMEM((2 * RANK, rows), bf16),
            pltpu.VMEM(up_map.shape[1:], bf16),
            pltpu.VMEM((tiles, 2 * RANK, 2 * LANES), bf16),
            pltpu.VMEM((tiles, rows, 2 * LANES), bf16),
            pltpu.SemaphoreType.DMA((3,)),
            pltpu.SemaphoreType.DMA((rows // BLOCK,)),
            pltpu.SemaphoreType.DMA((rows // BLOCK,)),
        ],
        compiler_params=params(56),
        cost_estimate=pl.CostEstimate(flops=4 * 10**9, bytes_accessed=20 * 10**6, transcendentals=0),
    )(codes, scale, down_map[0].T, up_map, before, held)


class Leave:
    def __init__(self, first, codes, scale, down_map, up_map, scratch):
        self.words, self.scale, self.down, self.up, self.sems = scratch
        self.first = first
        self.columns = self.words.shape[1]
        self.pairs = [
            (codes.at[0, :, pl.ds(first, self.columns)], self.words),
            (scale.at[0], self.scale),
            (down_map, self.down),
            (up_map.at[0], self.up),
        ]

    @staticmethod
    def scratch(columns, codes, scale, up_map):
        third = codes.shape[1]
        return [
            pltpu.VMEM((third, columns), jnp.int32),
            pltpu.VMEM(scale.shape[1:], bf16),
            pltpu.VMEM((RANK, 3 * third), bf16),
            pltpu.VMEM(up_map.shape[1:], bf16),
            pltpu.SemaphoreType.DMA((4,)),
        ]

    def start(self):
        self.moves = [copy(a, b, self.sems.at[i]) for i, (a, b) in enumerate(self.pairs)]

    def ready(self):
        for move in self.moves:
            move.wait()

    def decode(self, tables, strip, strips, weights, at):
        rows = self.words.shape[0]
        strip = strip * LANES if isinstance(strip, int) else pl.multiple_of(strip * LANES, LANES)
        adapter = lax.dot_general(
            self.down[...],
            self.up[:, pl.ds(self.first + strip, strips * LANES)],
            (((0,), (0,)), ((), ())),
            preferred_element_type=f32,
        ) * adapter_scale
        for j in range(strips):
            here = pl.ds(strip + j * LANES, LANES)
            there = pl.ds(self.first + strip + j * LANES, LANES)
            target = pl.ds(at + strip + j * LANES, LANES)
            for nibble in range(3):
                for g in range(rows // GROUP):
                    row = nibble * rows + g * GROUP
                    packed = self.words[pl.ds(g * GROUP, GROUP), here]
                    factor = self.scale[pl.ds(row // GROUP, 1), there].astype(f32)
                    value = decode(tables, packed, nibble) * factor
                    value = value + adapter[row : row + GROUP, j * LANES : (j + 1) * LANES]
                    weights[pl.ds(row, GROUP), target] = value.astype(bf16)


def leave_kernel(codes, scale, down_map, up_map, before, out, made, weights, out_sem, *scratch):
    leave = Leave(0, codes, scale, down_map, up_map, scratch)
    leave.start()
    made[...] = jnp.zeros_like(made)
    tables = level_tables()
    leave.ready()
    blocks = leave.columns // BLOCK

    def leaving(k):
        here = pl.ds(pl.multiple_of(k * BLOCK, BLOCK), BLOCK)
        return pltpu.make_async_copy(weights.at[:, here], out.at[:, here], out_sem.at[k])

    @pl.loop(0, blocks)
    def _(k):
        leave.decode(tables, k * (BLOCK // LANES), BLOCK // LANES, weights, 0)
        leaving(k).start()

    @pl.loop(0, blocks)
    def _(k):
        leaving(k).wait()


def leave_weights(columns, codes, scale, down_map, up_map, before):
    rows = 3 * codes.shape[1]
    return pl.pallas_call(
        leave_kernel,
        in_specs=in_hbm(4) + [pl.BlockSpec(memory_space=pl.ANY)],
        out_specs=in_hbm(1) + [pl.BlockSpec(memory_space=pltpu.VMEM)],
        out_shape=[jax.ShapeDtypeStruct((rows, columns), bf16), jax.ShapeDtypeStruct((8, LANES), f32)],
        scratch_shapes=[pltpu.VMEM((rows, columns), bf16), pltpu.SemaphoreType.DMA((columns // BLOCK,))]
        + Leave.scratch(columns, codes, scale, up_map),
        compiler_params=params(54),
        cost_estimate=pl.CostEstimate(flops=2 * 10**9, bytes_accessed=8 * 10**6, transcendentals=0),
    )(codes, scale, down_map[0].T, up_map, before)


def pick_rows(own, tables, rows, slots):
    cap = rows // 2
    total = rows * len(tables)
    lane = lax.broadcasted_iota(jnp.int32, (rows, LANES), 1)
    columns = []
    for shift in (0, LANES // 2):
        parts = [
            jnp.sum(jnp.where(lane == own + shift, t, 0.0), axis=-1, keepdims=True) for t in tables
        ]
        column = jnp.concatenate(parts, axis=0)
        columns.append(jnp.broadcast_to(column, (total, slots)))
    high, low = columns
    hit = (high != 0.0).astype(f32).astype(bf16)
    high, low = high.astype(bf16), low.astype(bf16)
    row = lax.broadcasted_iota(jnp.int32, (total, total), 0)
    column = lax.broadcasted_iota(jnp.int32, (total, total), 1)
    before = ((row // rows == column // rows) & (row < column)).astype(f32).astype(bf16)
    first = (((0,), (0,)), ((), ()))
    rank_of = lax.dot_general(hit, before, first, preferred_element_type=f32)
    hit_of = lax.dot_general(hit, unit(total), first, preferred_element_type=f32)
    slot = lax.broadcasted_iota(jnp.int32, (slots, total), 0)
    place = lax.broadcasted_iota(jnp.int32, (slots, total), 1)
    taken = (slot // cap == place // rows) & (rank_of == (slot % cap).astype(f32)) & (hit_of > 0.5)
    gather = taken.astype(f32).astype(bf16)
    weight = jnp.dot(gather, high, preferred_element_type=f32)
    weight = weight + jnp.dot(gather, low, preferred_element_type=f32)
    rank = lax.dot_general(before, hit, first, preferred_element_type=f32)
    slot = lax.broadcasted_iota(jnp.int32, (total, slots), 1)
    place = lax.broadcasted_iota(jnp.int32, (total, slots), 0)
    taken = (slot // cap == place // rows) & (rank == (slot % cap).astype(f32)) & (hit.astype(f32) > 0.5)
    return gather, taken.astype(f32).astype(bf16), weight


def expert_kernel(count, own, *refs):
    blocks, refs = refs[:count], refs[count:]
    enter, made, codes, scale, down_map, up_map = refs[:6]
    outs, refs = refs[6 : count + 6], refs[count + 6 :]
    rows_of, picked, spread, weight, active, enter_of, leave_of, rows_sem, enter_sem, made_sem = refs[:10]
    rows = blocks[0].shape[0]
    arriving_rows = [
        copy(blocks[r], rows_of.at[pl.ds(r * rows, rows)], rows_sem.at[r]) for r in range(count)
    ]
    begin = made.shape[1]
    leave = Leave(begin, codes, scale, down_map, up_map, refs[10:])
    leave.start()
    width = picked.shape[1]
    sets, span, slots = spread.shape
    tiles = enter_of.shape[0]
    each = count // sets
    wide = 8 * LANES

    def arriving(tile):
        return pltpu.make_async_copy(enter.at[tile], enter_of.at[tile], enter_sem.at[tile])

    for tile in range(FLYING):
        arriving(tile).start()
    made_move = copy(made, leave_of.at[:, pl.ds(0, begin)], made_sem)
    for move in arriving_rows:
        move.wait()
    for g in range(sets):
        tables = [
            rows_of[pl.ds(g * span + b * rows, rows), pl.ds(width, LANES)].astype(f32) for b in range(each)
        ]
        gather, scatter, factor = pick_rows(own[0], tables, rows, slots)
        here = pl.ds(g * slots, slots)
        spread[g] = scatter
        weight[here, :] = factor
        for n in range(width // wide):
            lanes = pl.ds(n * wide, wide)
            source = rows_of[pl.ds(g * span, span), lanes]
            picked[here, lanes] = jnp.dot(gather, source, preferred_element_type=f32).astype(bf16)
    levels = level_tables()
    leave.ready()
    strips = leave.columns // LANES
    per_tile = strips // tiles

    @pl.loop(0, tiles)
    def _(tile):
        arriving(tile).wait()

        @pl.when(tile + FLYING < tiles)
        def _():
            arriving(tile + FLYING).start()

        joined = jnp.dot(picked[...], enter_of[tile], preferred_element_type=f32)
        leave.decode(levels, tile * per_tile, per_tile, leave_of, begin)
        gate = joined[:, :LANES]
        value = gate / (1.0 + jnp.exp(-gate)) * joined[:, LANES:]
        active[tile] = value.astype(bf16)

    if tiles * per_tile < strips:
        leave.decode(levels, tiles * per_tile, strips - tiles * per_tile, leave_of, begin)
    made_move.wait()

    @pl.loop(0, width // wide)
    def _(n):
        lanes = pl.ds(pl.multiple_of(n * wide, wide), wide)
        entry = jnp.concatenate([active[t] for t in range(tiles)], axis=1)
        factor = jnp.concatenate([weight[...]] * (wide // slots), axis=1)
        result = jnp.dot(entry, leave_of[:, lanes], preferred_element_type=f32)
        result = (result * factor).astype(bf16)
        for g in range(sets):
            own_rows = result[g * slots : (g + 1) * slots]
            full = jnp.dot(spread[g], own_rows, preferred_element_type=f32).astype(bf16)
            for b in range(each):
                outs[g * each + b][:, lanes] = full[b * rows : (b + 1) * rows]


def expert(own, blocks, enter, made, codes, scale, down_map, up_map):
    count = len(blocks)
    tiles = enter.shape[0]
    rows, padded = blocks[0].shape
    width = padded - LANES
    each = LANES // (rows // 2)
    sets = count // each
    vmem = pl.BlockSpec(memory_space=pltpu.VMEM)
    return pl.pallas_call(
        functools.partial(expert_kernel, count),
        in_specs=[pl.BlockSpec(memory_space=pltpu.SMEM)]
        + in_hbm(count + 6),
        out_specs=[vmem] * count,
        out_shape=[jax.ShapeDtypeStruct((rows, width), bf16)] * count,
        scratch_shapes=[
            pltpu.VMEM((count * rows, padded), bf16),
            pltpu.VMEM((sets * LANES, width), bf16),
            pltpu.VMEM((sets, each * rows, LANES), bf16),
            pltpu.VMEM((sets * LANES, LANES), f32),
            pltpu.VMEM((tiles, sets * LANES, LANES), bf16),
            pltpu.VMEM(enter.shape, bf16),
            pltpu.VMEM((made.shape[0], width), bf16),
            pltpu.SemaphoreType.DMA((count,)),
            pltpu.SemaphoreType.DMA((tiles,)),
            pltpu.SemaphoreType.DMA,
        ]
        + Leave.scratch(width - made.shape[1], codes, scale, up_map),
        compiler_params=params(48),
        cost_estimate=pl.CostEstimate(flops=8 * 10**9, bytes_accessed=22 * 10**6, transcendentals=0),
    )(own, *blocks, enter, made, codes, scale, down_map[0].T, up_map)


def attend_kernel(
    lengths, queries, fresh, cache, _, out, queries_of, fresh_of, cache_of, small_sem, cache_sem, *, first, block
):
    rows = out.shape[0]
    mine = pl.ds(first, rows)
    scaling = 1.0 / math.sqrt(HEAD)
    positions = cache.shape[2]
    small = [copy(queries.at[mine], queries_of, small_sem.at[0]), copy(fresh.at[mine], fresh_of, small_sem.at[1])]

    def arriving(k):
        there = pl.ds(first + k * block, block)
        return pltpu.make_async_copy(cache.at[there], cache_of.at[pl.ds(k * block, block)], cache_sem.at[k])

    for k in range(rows // block):
        arriving(k).start()
    lower = lax.broadcasted_iota(jnp.int32, (HEADS, HEAD), 0) < HEADS // KV_HEADS
    place = lax.broadcasted_iota(jnp.int32, (HEADS, positions), 1)
    own_half = lambda both: jnp.where(lower, both[:, :HEAD], both[:, HEAD:])
    for move in small:
        move.wait()

    @pl.loop(0, rows // block)
    def _(k):
        arriving(k).wait()
        old, new = [], []
        for t in range(block):
            row = k * block + t
            query = queries_of[row]
            zero = jnp.zeros_like(query)
            both = jnp.concatenate([jnp.where(lower, query, zero), jnp.where(lower, zero, query)], axis=1)
            score = lax.dot_general(
                both, cache_of[row, 0], (((1,), (1,)), ((), ())), preferred_element_type=f32
            )
            old.append(jnp.where(place < lengths[first + row], score * scaling, -jnp.inf))
            key = own_half(fresh_of[row, 0:1, :].astype(f32))
            new.append(jnp.sum(query.astype(f32) * key, axis=-1, keepdims=True) * scaling)
        old, new = jnp.concatenate(old, axis=0), jnp.concatenate(new, axis=0)
        highest = jnp.maximum(jnp.max(old, axis=-1, keepdims=True), new)
        old = jnp.exp(old - highest)
        new = jnp.exp(new - highest)
        inverse = 1.0 / (jnp.sum(old, axis=-1, keepdims=True) + new)
        old = (old * inverse).astype(bf16)
        new = (new * inverse).astype(bf16).astype(f32)
        for t in range(block):
            row = k * block + t
            heads = slice(t * HEADS, (t + 1) * HEADS)
            blended = own_half(jnp.dot(old[heads], cache_of[row, 1], preferred_element_type=f32))
            out[row] = (blended + new[heads] * own_half(fresh_of[row, 1:2, :].astype(f32))).astype(bf16)


def attend(queries, fresh_key_value, key_value_cache, lengths, before, part, parts, block=8):
    rows = queries.shape[0] // parts
    return pl.pallas_call(
        functools.partial(attend_kernel, first=part * rows, block=block),
        in_specs=[pl.BlockSpec(memory_space=pltpu.SMEM)] + in_hbm(3) + [pl.BlockSpec(memory_space=pl.ANY)],
        out_specs=pl.BlockSpec(memory_space=pltpu.VMEM),
        out_shape=jax.ShapeDtypeStruct((rows, HEADS, HEAD), bf16),
        scratch_shapes=[
            pltpu.VMEM((rows, HEADS, HEAD), bf16),
            pltpu.VMEM((rows, *fresh_key_value.shape[1:]), bf16),
            pltpu.VMEM((rows, *key_value_cache.shape[1:]), bf16),
            pltpu.SemaphoreType.DMA((2,)),
            pltpu.SemaphoreType.DMA((rows // block,)),
        ],
        compiler_params=params(49),
        cost_estimate=pl.CostEstimate(flops=5 * 10**8, bytes_accessed=20 * 10**6, transcendentals=0),
    )(lengths, queries, fresh_key_value, key_value_cache, before)


def swap(value, bit):
    count = lax.axis_size("ep")
    return lax.ppermute(value, "ep", [(i, i ^ bit) for i in range(count)])


def add(terms):
    return sum(term.astype(f32) for term in terms[1:]) + terms[0].astype(f32)


def shards(
    queries,
    fresh_key_value,
    key_value_cache,
    lengths,
    hidden,
    expert_norm_gain,
    routes,
    router_scores,
    gate_up_quant_codes,
    gate_up_code_scale,
    down_quant_codes,
    down_code_scale,
    adapter_input_down,
    adapter_input_up,
    adapter_output_down,
    adapter_output_up,
):
    count = lax.axis_size("ep")
    bits = [1 << b for b in range(count.bit_length() - 1)]
    rows = hidden.shape[0]
    blocks = {0: norm_rows(hidden, expert_norm_gain, routes, router_scores)}
    leave_args = (down_quant_codes, down_code_scale, adapter_output_down, adapter_output_up)

    heads = queries.reshape(rows, HEADS, HEAD)
    attention = functools.partial(attend, heads, fresh_key_value, key_value_cache, lengths, parts=2)

    def make_enter(part, before, held):
        return enter_weights(
            part, 2, gate_up_quant_codes, gate_up_code_scale, adapter_input_down, adapter_input_up, before, held
        )

    stage = lambda r: sum(1 for bit in bits[1:] if r & bit)
    low_bit = lambda r: r & -r
    even = [r for r in range(count) if r and r % 2 == 0]
    done = blocks[0]
    for now in range(max(stage(r) for r in even) + 1):
        for r in sorted(even, key=low_bit, reverse=True):
            if stage(r ^ low_bit(r)) == now:
                blocks[r] = swap(blocks[r ^ low_bit(r)], low_bit(r))
        for r in [0] + even:
            if stage(r) == now:
                blocks[r | 1] = swap(blocks[r], 1)
        arriving = [r for r in blocks if r % 2 == 0 and stage(r) == now + 1]
        held = [blocks[r] for r in arriving]
        if now < 2:
            weights, done = make_enter(now, done, weights if now else done)
        elif now == 2:
            others = [r | 1 for r in even if stage(r) == now]
            done, *swapped = lax.optimization_barrier((done, *[blocks[r] for r in others]))
            blocks.update(zip(others, swapped))
            first_columns, done = leave_weights(hidden.shape[1] // 2, *leave_args, done)
        if now == 2:
            *held, first_columns = lax.optimization_barrier((*held, first_columns))
        else:
            *held, done = lax.optimization_barrier((*held, done))
        blocks.update(zip(arriving, held))
    own = lax.axis_index("ep").astype(jnp.int32).reshape(1)
    produced = expert(own, [blocks[r] for r in range(count)], weights, first_columns, *leave_args)

    tie = lambda *values: list(lax.optimization_barrier(values))
    sums = {r: [produced[r]] for r in range(0, count, 2)}
    first = count - 2
    sent = add([sums.pop(first)[0], swap(produced[first + 1], 1)]).astype(bf16)
    sent, *others = tie(sent, *[produced[r + 1] for r in sums])
    arrived = swap(sent, bits[1])
    for r, value in zip(sums, others):
        sums[r].append(swap(value, 1))
    early = (first - 2, first - 4)
    before, *held = tie(sent, *[sums[r][1] for r in early])
    for r, value in zip(early, held):
        sums[r][1] = value
    context = attention(before, 0)
    arrived, context = tie(arrived, context)
    sums[first ^ bits[1]].append(arrived)
    for r in range(first - 2, 0, -4):
        pair = tie(*[add(sums.pop(q)).astype(bf16) for q in (r, r - 2)])
        for q, value in zip((r, r - 2), pair):
            sums[q ^ low_bit(q)].append(swap(value, low_bit(q)))
    later = attention(pair[1], 1)
    context = jnp.concatenate([context, later]).reshape(rows, HEADS * HEAD)
    return (context, add(sums[0]).astype(bf16))


def solution(mesh):
    return jax.shard_map(
        shards,
        mesh=mesh,
        in_specs=(
            P(("grp", "ep"), None),
            P(("grp", "ep"), None, None),
            P(("grp", "ep"), None, None, None),
            P(("grp", "ep")),
            P(("grp", "ep"), None),
            P(),
            P(("grp", "ep"), None),
            P(("grp", "ep"), None),
            P("ep", None, None),
            P("ep", None, None),
            P("ep", None, None),
            P("ep", None, None),
            P("ep", None, None),
            P("ep", None, None, None),
            P("ep", None, None),
            P("ep", None, None),
        ),
        out_specs=(P(("grp", "ep"), None), P(("grp", "ep"), None)),
        check_vma=False,
    )
```

```python
import functools
import math

import jax
import jax.numpy as jnp
from jax import lax
from jax.experimental import pallas as pl
from jax.experimental.pallas import tpu as pltpu
from jax.sharding import PartitionSpec as P

HEADS = 32
KV_HEADS = 2
HEAD = 128
RANK = 16
LANES = 128
GROUP = 64
FLYING = 6
AHEAD = 2
BLOCK = 512
code_levels = (
    -1.0,
    -0.6961928009986877,
    -0.5250730514526367,
    -0.39491748809814453,
    -0.28444138169288635,
    -0.18477343022823334,
    -0.09105003625154495,
    0.0,
    0.07958029955625534,
    0.16093020141124725,
    0.24611230194568634,
    0.33791524171829224,
    0.44070982933044434,
    0.5626170039176941,
    0.7229568362236023,
    1.0,
)
adapter_scale = 2.0
norm_epsilon = 1e-06
f32 = jnp.float32
bf16 = jnp.bfloat16


def params(mib):
    return pltpu.CompilerParams(vmem_limit_bytes=mib * 2**20)


def whole(shape):
    return pl.BlockSpec(shape, lambda *_: (0,) * len(shape))


def norm_kernel(hidden, gain, routes, scores, out):
    rows, width = hidden.shape
    wide = hidden[...].astype(f32)
    spread = jnp.mean(wide * wide, axis=-1, keepdims=True)
    normed = wide * lax.rsqrt(spread + norm_epsilon) * gain[...].astype(f32).reshape(1, width)
    out[:, :width] = normed.astype(bf16)
    logits = scores[...]
    parts = jnp.exp(logits - jnp.max(logits, axis=0, keepdims=True))
    shares = parts / jnp.sum(parts, axis=0, keepdims=True)
    place = lax.broadcasted_iota(jnp.int32, (LANES, rows), 0)
    named = place & (LANES // 2 - 1)
    table = jnp.zeros((LANES, rows), f32)
    for k in range(routes.shape[0]):
        table = table + jnp.where(routes[k : k + 1, :] == named, shares[k : k + 1, :], 0.0)
    high = table.astype(bf16).astype(f32)
    both = jnp.where(place < LANES // 2, high, table - high).astype(bf16)
    out[:, width:] = lax.dot_general(
        unit(rows), both, (((1,), (1,)), ((), ())), preferred_element_type=f32
    ).astype(bf16)


def unit(size):
    row = lax.broadcasted_iota(jnp.int32, (size, size), 0)
    return (row == lax.broadcasted_iota(jnp.int32, (size, size), 1)).astype(f32).astype(bf16)


def norm_rows(hidden, gain, routes, scores):
    rows, width = hidden.shape
    top = routes.shape[1]
    return pl.pallas_call(
        norm_kernel,
        grid=(1,),
        in_specs=[whole((rows, width)), whole((width,)), whole((top, rows)), whole((top, rows))],
        out_specs=whole((rows, width + LANES)),
        out_shape=jax.ShapeDtypeStruct((rows, width + LANES), bf16),
        compiler_params=params(56),
    )(hidden, gain, routes.T, scores.T)


def level_tables():
    sub = lax.broadcasted_iota(jnp.int32, (8, LANES), 0)
    low = jnp.zeros((8, LANES), f32)
    high = low
    for i in range(8):
        low = jnp.where(sub == i, code_levels[i], low)
        high = jnp.where(sub == i, code_levels[i + 8], high)
    return low, high


def decode(tables, words, nibble):
    pieces = []
    for q in range(words.shape[0] // 8):
        word = words[8 * q : 8 * q + 8]
        entry = (word >> (4 * nibble)) & 7
        upper = (word & (8 << (4 * nibble))) != 0
        low = jnp.take_along_axis(tables[0], entry, axis=0, mode="promise_in_bounds")
        high = jnp.take_along_axis(tables[1], entry, axis=0, mode="promise_in_bounds")
        pieces.append(jnp.where(upper, high, low))
    return jnp.concatenate(pieces, axis=0)


def copy(source, target, sem):
    move = pltpu.make_async_copy(source, target, sem)
    move.start()
    return move


def enter_kernel(
    part, rows, codes, scale, down_map, up_map, before, held, out, made,
    words_of, scale_of, factors, down_of, up_of, spread, weights, small_sem, in_sem, out_sem,
):
    tiles = out.shape[0]
    third = codes.shape[2]
    half = tiles * LANES
    first = part * rows
    blocks = rows // BLOCK
    arriving = [
        copy(scale.at[0, pl.ds(first // GROUP, rows // GROUP)], scale_of, small_sem.at[0]),
        copy(down_map.at[:, pl.ds(first, rows)], down_of, small_sem.at[1]),
        copy(up_map.at[0], up_of, small_sem.at[2]),
    ]

    def arriving_words(k):
        here = pl.multiple_of(k * BLOCK, BLOCK)
        return pltpu.make_async_copy(
            codes.at[0, pl.ds(first + here, BLOCK)], words_of.at[pl.ds(here, BLOCK)], in_sem.at[k]
        )

    for k in range(AHEAD):
        arriving_words(k).start()
    made[...] = jnp.zeros_like(made)
    tables = level_tables()
    spread[...] = jnp.zeros_like(spread)
    for move in arriving:
        move.wait()
    for tile in range(tiles):
        for side in range(2):
            piece = up_of[side, :, tile * LANES : (tile + 1) * LANES].astype(f32) * adapter_scale
            spread[tile, side * RANK : (side + 1) * RANK, side * LANES : (side + 1) * LANES] = piece.astype(bf16)
    factors[...] = scale_of[...].astype(f32)
    scales = BLOCK // GROUP

    def leaving(k):
        here = pl.ds(pl.multiple_of(k * BLOCK, BLOCK), BLOCK)
        there = pl.ds(pl.multiple_of(first + k * BLOCK, BLOCK), BLOCK)
        return pltpu.make_async_copy(weights.at[:, here], out.at[:, there], out_sem.at[k])

    @pl.loop(0, blocks)
    def _(k):
        arriving_words(k).wait()

        @pl.when(k + AHEAD < blocks)
        def _():
            arriving_words(k + AHEAD).start()

        here = pl.multiple_of(k * BLOCK, BLOCK)
        for tile in range(tiles):
            adapter = lax.dot_general(
                down_of[:, pl.ds(here, BLOCK)],
                spread[tile],
                (((0,), (0,)), ((), ())),
                preferred_element_type=f32,
            )
            for side in range(2):
                column = side * half + tile * LANES
                nibble, offset = divmod(column, third)
                factor = factors[pl.ds(pl.multiple_of(k * scales, scales), scales), pl.ds(column, LANES)]
                for g in range(scales):
                    packed = words_of[pl.ds(here + g * GROUP, GROUP), pl.ds(offset, LANES)]
                    value = decode(tables, packed, nibble) * factor[g : g + 1]
                    value = value + adapter[g * GROUP : (g + 1) * GROUP, side * LANES : (side + 1) * LANES]
                    weights[tile, pl.ds(here + g * GROUP, GROUP), pl.ds(side * LANES, LANES)] = value.astype(bf16)
        leaving(k).start()

    @pl.loop(0, blocks)
    def _(k):
        leaving(k).wait()


def in_hbm(count):
    return [pl.BlockSpec(memory_space=pltpu.HBM)] * count


def enter_weights(part, parts, codes, scale, down_map, up_map, before, held):
    _, width, third = codes.shape
    tiles = 3 * third // 2 // LANES
    rows = width // parts
    return pl.pallas_call(
        functools.partial(enter_kernel, part, rows),
        in_specs=in_hbm(4) + [pl.BlockSpec(memory_space=pl.ANY)] * 2,
        out_specs=in_hbm(1) + [pl.BlockSpec(memory_space=pltpu.VMEM)],
        input_output_aliases={5: 0} if part else {},
        out_shape=[
            jax.ShapeDtypeStruct((tiles, width, 2 * LANES), bf16),
            jax.ShapeDtypeStruct((8, LANES), f32),
        ],
        scratch_shapes=[
            pltpu.VMEM((rows, third), jnp.int32),
            pltpu.VMEM((rows // GROUP, 3 * third), bf16),
            pltpu.VMEM((rows // GROUP, 3 * third), f32),
            pltpu.VMEM((2 * RANK, rows), bf16),
            pltpu.VMEM(up_map.shape[1:], bf16),
            pltpu.VMEM((tiles, 2 * RANK, 2 * LANES), bf16),
            pltpu.VMEM((tiles, rows, 2 * LANES), bf16),
            pltpu.SemaphoreType.DMA((3,)),
            pltpu.SemaphoreType.DMA((rows // BLOCK,)),
            pltpu.SemaphoreType.DMA((rows // BLOCK,)),
        ],
        compiler_params=params(56),
        cost_estimate=pl.CostEstimate(flops=4 * 10**9, bytes_accessed=20 * 10**6, transcendentals=0),
    )(codes, scale, down_map[0].T, up_map, before, held)


class Leave:
    def __init__(self, first, codes, scale, down_map, up_map, scratch):
        self.words, self.scale, self.down, self.up, self.sems = scratch
        self.first = first
        self.columns = self.words.shape[1]
        self.pairs = [
            (codes.at[0, :, pl.ds(first, self.columns)], self.words),
            (scale.at[0], self.scale),
            (down_map, self.down),
            (up_map.at[0], self.up),
        ]

    @staticmethod
    def scratch(columns, codes, scale, up_map):
        third = codes.shape[1]
        return [
            pltpu.VMEM((third, columns), jnp.int32),
            pltpu.VMEM(scale.shape[1:], bf16),
            pltpu.VMEM((RANK, 3 * third), bf16),
            pltpu.VMEM(up_map.shape[1:], bf16),
            pltpu.SemaphoreType.DMA((4,)),
        ]

    def start(self):
        self.moves = [copy(a, b, self.sems.at[i]) for i, (a, b) in enumerate(self.pairs)]

    def ready(self):
        for move in self.moves:
            move.wait()

    def decode(self, tables, strip, strips, weights, at):
        rows = self.words.shape[0]
        strip = strip * LANES if isinstance(strip, int) else pl.multiple_of(strip * LANES, LANES)
        adapter = lax.dot_general(
            self.down[...],
            self.up[:, pl.ds(self.first + strip, strips * LANES)],
            (((0,), (0,)), ((), ())),
            preferred_element_type=f32,
        ) * adapter_scale
        for j in range(strips):
            here = pl.ds(strip + j * LANES, LANES)
            there = pl.ds(self.first + strip + j * LANES, LANES)
            target = pl.ds(at + strip + j * LANES, LANES)
            for nibble in range(3):
                for g in range(rows // GROUP):
                    row = nibble * rows + g * GROUP
                    packed = self.words[pl.ds(g * GROUP, GROUP), here]
                    factor = self.scale[pl.ds(row // GROUP, 1), there].astype(f32)
                    value = decode(tables, packed, nibble) * factor
                    value = value + adapter[row : row + GROUP, j * LANES : (j + 1) * LANES]
                    weights[pl.ds(row, GROUP), target] = value.astype(bf16)


def leave_kernel(codes, scale, down_map, up_map, before, out, made, weights, out_sem, *scratch):
    leave = Leave(0, codes, scale, down_map, up_map, scratch)
    leave.start()
    made[...] = jnp.zeros_like(made)
    tables = level_tables()
    leave.ready()
    blocks = leave.columns // BLOCK

    def leaving(k):
        here = pl.ds(pl.multiple_of(k * BLOCK, BLOCK), BLOCK)
        return pltpu.make_async_copy(weights.at[:, here], out.at[:, here], out_sem.at[k])

    @pl.loop(0, blocks)
    def _(k):
        leave.decode(tables, k * (BLOCK // LANES), BLOCK // LANES, weights, 0)
        leaving(k).start()

    @pl.loop(0, blocks)
    def _(k):
        leaving(k).wait()


def leave_weights(columns, codes, scale, down_map, up_map, before):
    rows = 3 * codes.shape[1]
    return pl.pallas_call(
        leave_kernel,
        in_specs=in_hbm(4) + [pl.BlockSpec(memory_space=pl.ANY)],
        out_specs=in_hbm(1) + [pl.BlockSpec(memory_space=pltpu.VMEM)],
        out_shape=[jax.ShapeDtypeStruct((rows, columns), bf16), jax.ShapeDtypeStruct((8, LANES), f32)],
        scratch_shapes=[pltpu.VMEM((rows, columns), bf16), pltpu.SemaphoreType.DMA((columns // BLOCK,))]
        + Leave.scratch(columns, codes, scale, up_map),
        compiler_params=params(54),
        cost_estimate=pl.CostEstimate(flops=2 * 10**9, bytes_accessed=8 * 10**6, transcendentals=0),
    )(codes, scale, down_map[0].T, up_map, before)


def pick_rows(own, tables, rows, slots):
    cap = rows // 2
    total = rows * len(tables)
    lane = lax.broadcasted_iota(jnp.int32, (rows, LANES), 1)
    columns = []
    for shift in (0, LANES // 2):
        parts = [
            jnp.sum(jnp.where(lane == own + shift, t, 0.0), axis=-1, keepdims=True) for t in tables
        ]
        column = jnp.concatenate(parts, axis=0)
        columns.append(jnp.broadcast_to(column, (total, slots)))
    high, low = columns
    hit = (high != 0.0).astype(f32).astype(bf16)
    high, low = high.astype(bf16), low.astype(bf16)
    row = lax.broadcasted_iota(jnp.int32, (total, total), 0)
    column = lax.broadcasted_iota(jnp.int32, (total, total), 1)
    before = ((row // rows == column // rows) & (row < column)).astype(f32).astype(bf16)
    first = (((0,), (0,)), ((), ()))
    rank_of = lax.dot_general(hit, before, first, preferred_element_type=f32)
    hit_of = lax.dot_general(hit, unit(total), first, preferred_element_type=f32)
    slot = lax.broadcasted_iota(jnp.int32, (slots, total), 0)
    place = lax.broadcasted_iota(jnp.int32, (slots, total), 1)
    taken = (slot // cap == place // rows) & (rank_of == (slot % cap).astype(f32)) & (hit_of > 0.5)
    gather = taken.astype(f32).astype(bf16)
    weight = jnp.dot(gather, high, preferred_element_type=f32)
    weight = weight + jnp.dot(gather, low, preferred_element_type=f32)
    rank = lax.dot_general(before, hit, first, preferred_element_type=f32)
    slot = lax.broadcasted_iota(jnp.int32, (total, slots), 1)
    place = lax.broadcasted_iota(jnp.int32, (total, slots), 0)
    taken = (slot // cap == place // rows) & (rank == (slot % cap).astype(f32)) & (hit.astype(f32) > 0.5)
    return gather, taken.astype(f32).astype(bf16), weight


def expert_kernel(count, own, *refs):
    blocks, refs = refs[:count], refs[count:]
    enter, made, codes, scale, down_map, up_map = refs[:6]
    outs, refs = refs[6 : count + 6], refs[count + 6 :]
    rows_of, picked, spread, weight, active, enter_of, leave_of, rows_sem, enter_sem, made_sem = refs[:10]
    rows = blocks[0].shape[0]
    arriving_rows = [
        copy(blocks[r], rows_of.at[pl.ds(r * rows, rows)], rows_sem.at[r]) for r in range(count)
    ]
    begin = made.shape[1]
    leave = Leave(begin, codes, scale, down_map, up_map, refs[10:])
    leave.start()
    width = picked.shape[1]
    sets, span, slots = spread.shape
    tiles = enter_of.shape[0]
    each = count // sets
    wide = 8 * LANES

    def arriving(tile):
        return pltpu.make_async_copy(enter.at[tile], enter_of.at[tile], enter_sem.at[tile])

    for tile in range(FLYING):
        arriving(tile).start()
    made_move = copy(made, leave_of.at[:, pl.ds(0, begin)], made_sem)
    for move in arriving_rows:
        move.wait()
    for g in range(sets):
        tables = [
            rows_of[pl.ds(g * span + b * rows, rows), pl.ds(width, LANES)].astype(f32) for b in range(each)
        ]
        gather, scatter, factor = pick_rows(own[0], tables, rows, slots)
        here = pl.ds(g * slots, slots)
        spread[g] = scatter
        weight[here, :] = factor
        for n in range(width // wide):
            lanes = pl.ds(n * wide, wide)
            source = rows_of[pl.ds(g * span, span), lanes]
            picked[here, lanes] = jnp.dot(gather, source, preferred_element_type=f32).astype(bf16)
    levels = level_tables()
    leave.ready()
    strips = leave.columns // LANES
    per_tile = strips // tiles

    @pl.loop(0, tiles)
    def _(tile):
        arriving(tile).wait()

        @pl.when(tile + FLYING < tiles)
        def _():
            arriving(tile + FLYING).start()

        joined = jnp.dot(picked[...], enter_of[tile], preferred_element_type=f32)
        leave.decode(levels, tile * per_tile, per_tile, leave_of, begin)
        gate = joined[:, :LANES]
        value = gate / (1.0 + jnp.exp(-gate)) * joined[:, LANES:]
        active[tile] = value.astype(bf16)

    if tiles * per_tile < strips:
        leave.decode(levels, tiles * per_tile, strips - tiles * per_tile, leave_of, begin)
    made_move.wait()

    @pl.loop(0, width // wide)
    def _(n):
        lanes = pl.ds(pl.multiple_of(n * wide, wide), wide)
        entry = jnp.concatenate([active[t] for t in range(tiles)], axis=1)
        factor = jnp.concatenate([weight[...]] * (wide // slots), axis=1)
        result = jnp.dot(entry, leave_of[:, lanes], preferred_element_type=f32)
        result = (result * factor).astype(bf16)
        for g in range(sets):
            own_rows = result[g * slots : (g + 1) * slots]
            full = jnp.dot(spread[g], own_rows, preferred_element_type=f32).astype(bf16)
            for b in range(each):
                outs[g * each + b][:, lanes] = full[b * rows : (b + 1) * rows]


def expert(own, blocks, enter, made, codes, scale, down_map, up_map):
    count = len(blocks)
    tiles = enter.shape[0]
    rows, padded = blocks[0].shape
    width = padded - LANES
    each = LANES // (rows // 2)
    sets = count // each
    vmem = pl.BlockSpec(memory_space=pltpu.VMEM)
    return pl.pallas_call(
        functools.partial(expert_kernel, count),
        in_specs=[pl.BlockSpec(memory_space=pltpu.SMEM)]
        + in_hbm(count + 6),
        out_specs=[vmem] * count,
        out_shape=[jax.ShapeDtypeStruct((rows, width), bf16)] * count,
        scratch_shapes=[
            pltpu.VMEM((count * rows, padded), bf16),
            pltpu.VMEM((sets * LANES, width), bf16),
            pltpu.VMEM((sets, each * rows, LANES), bf16),
            pltpu.VMEM((sets * LANES, LANES), f32),
            pltpu.VMEM((tiles, sets * LANES, LANES), bf16),
            pltpu.VMEM(enter.shape, bf16),
            pltpu.VMEM((made.shape[0], width), bf16),
            pltpu.SemaphoreType.DMA((count,)),
            pltpu.SemaphoreType.DMA((tiles,)),
            pltpu.SemaphoreType.DMA,
        ]
        + Leave.scratch(width - made.shape[1], codes, scale, up_map),
        compiler_params=params(48),
        cost_estimate=pl.CostEstimate(flops=8 * 10**9, bytes_accessed=22 * 10**6, transcendentals=0),
    )(own, *blocks, enter, made, codes, scale, down_map[0].T, up_map)


def attend_kernel(
    lengths, queries, fresh, cache, _, out, queries_of, fresh_of, cache_of, small_sem, cache_sem, *, first, block
):
    rows = out.shape[0]
    mine = pl.ds(first, rows)
    scaling = 1.0 / math.sqrt(HEAD)
    positions = cache.shape[2]
    small = [copy(queries.at[mine], queries_of, small_sem.at[0]), copy(fresh.at[mine], fresh_of, small_sem.at[1])]

    def arriving(k):
        there = pl.ds(first + k * block, block)
        return pltpu.make_async_copy(cache.at[there], cache_of.at[pl.ds(k * block, block)], cache_sem.at[k])

    for k in range(rows // block):
        arriving(k).start()
    lower = lax.broadcasted_iota(jnp.int32, (HEADS, HEAD), 0) < HEADS // KV_HEADS
    place = lax.broadcasted_iota(jnp.int32, (HEADS, positions), 1)
    own_half = lambda both: jnp.where(lower, both[:, :HEAD], both[:, HEAD:])
    for move in small:
        move.wait()

    @pl.loop(0, rows // block)
    def _(k):
        arriving(k).wait()
        old, new = [], []
        for t in range(block):
            row = k * block + t
            query = queries_of[row]
            zero = jnp.zeros_like(query)
            both = jnp.concatenate([jnp.where(lower, query, zero), jnp.where(lower, zero, query)], axis=1)
            score = lax.dot_general(
                both, cache_of[row, 0], (((1,), (1,)), ((), ())), preferred_element_type=f32
            )
            old.append(jnp.where(place < lengths[first + row], score * scaling, -jnp.inf))
            key = own_half(fresh_of[row, 0:1, :].astype(f32))
            new.append(jnp.sum(query.astype(f32) * key, axis=-1, keepdims=True) * scaling)
        old, new = jnp.concatenate(old, axis=0), jnp.concatenate(new, axis=0)
        highest = jnp.maximum(jnp.max(old, axis=-1, keepdims=True), new)
        old = jnp.exp(old - highest)
        new = jnp.exp(new - highest)
        inverse = 1.0 / (jnp.sum(old, axis=-1, keepdims=True) + new)
        old = (old * inverse).astype(bf16)
        new = (new * inverse).astype(bf16).astype(f32)
        for t in range(block):
            row = k * block + t
            heads = slice(t * HEADS, (t + 1) * HEADS)
            blended = own_half(jnp.dot(old[heads], cache_of[row, 1], preferred_element_type=f32))
            out[row] = (blended + new[heads] * own_half(fresh_of[row, 1:2, :].astype(f32))).astype(bf16)


def attend(queries, fresh_key_value, key_value_cache, lengths, before, part, parts, block=8):
    rows = queries.shape[0] // parts
    return pl.pallas_call(
        functools.partial(attend_kernel, first=part * rows, block=block),
        in_specs=[pl.BlockSpec(memory_space=pltpu.SMEM)] + in_hbm(3) + [pl.BlockSpec(memory_space=pl.ANY)],
        out_specs=pl.BlockSpec(memory_space=pltpu.VMEM),
        out_shape=jax.ShapeDtypeStruct((rows, HEADS, HEAD), bf16),
        scratch_shapes=[
            pltpu.VMEM((rows, HEADS, HEAD), bf16),
            pltpu.VMEM((rows, *fresh_key_value.shape[1:]), bf16),
            pltpu.VMEM((rows, *key_value_cache.shape[1:]), bf16),
            pltpu.SemaphoreType.DMA((2,)),
            pltpu.SemaphoreType.DMA((rows // block,)),
        ],
        compiler_params=params(49),
        cost_estimate=pl.CostEstimate(flops=5 * 10**8, bytes_accessed=20 * 10**6, transcendentals=0),
    )(lengths, queries, fresh_key_value, key_value_cache, before)


def swap(value, bit):
    count = lax.axis_size("ep")
    return lax.ppermute(value, "ep", [(i, i ^ bit) for i in range(count)])


def add(terms):
    return sum(term.astype(f32) for term in terms[1:]) + terms[0].astype(f32)


def shards(
    queries,
    fresh_key_value,
    key_value_cache,
    lengths,
    hidden,
    expert_norm_gain,
    routes,
    router_scores,
    gate_up_quant_codes,
    gate_up_code_scale,
    down_quant_codes,
    down_code_scale,
    adapter_input_down,
    adapter_input_up,
    adapter_output_down,
    adapter_output_up,
):
    count = lax.axis_size("ep")
    bits = [1 << b for b in range(count.bit_length() - 1)]
    rows = hidden.shape[0]
    blocks = {0: norm_rows(hidden, expert_norm_gain, routes, router_scores)}
    leave_args = (down_quant_codes, down_code_scale, adapter_output_down, adapter_output_up)

    heads = queries.reshape(rows, HEADS, HEAD)
    attention = functools.partial(attend, heads, fresh_key_value, key_value_cache, lengths, parts=2)

    def make_enter(part, before, held):
        return enter_weights(
            part, 2, gate_up_quant_codes, gate_up_code_scale, adapter_input_down, adapter_input_up, before, held
        )

    stage = lambda r: sum(1 for bit in bits[1:] if r & bit)
    low_bit = lambda r: r & -r
    even = [r for r in range(count) if r and r % 2 == 0]
    done = blocks[0]
    for now in range(max(stage(r) for r in even) + 1):
        for r in sorted(even, key=low_bit, reverse=True):
            if stage(r ^ low_bit(r)) == now:
                blocks[r] = swap(blocks[r ^ low_bit(r)], low_bit(r))
        for r in [0] + even:
            if stage(r) == now:
                blocks[r | 1] = swap(blocks[r], 1)
        arriving = [r for r in blocks if r % 2 == 0 and stage(r) == now + 1]
        held = [blocks[r] for r in arriving]
        if now < 2:
            weights, done = make_enter(now, done, weights if now else done)
        elif now == 2:
            others = [r | 1 for r in even if stage(r) == now]
            done, *swapped = lax.optimization_barrier((done, *[blocks[r] for r in others]))
            blocks.update(zip(others, swapped))
            first_columns, done = leave_weights(hidden.shape[1] // 2, *leave_args, done)
        if now == 2:
            *held, first_columns = lax.optimization_barrier((*held, first_columns))
        else:
            *held, done = lax.optimization_barrier((*held, done))
        blocks.update(zip(arriving, held))
    own = lax.axis_index("ep").astype(jnp.int32).reshape(1)
    produced = expert(own, [blocks[r] for r in range(count)], weights, first_columns, *leave_args)

    tie = lambda *values: list(lax.optimization_barrier(values))
    sums = {r: [produced[r]] for r in range(0, count, 2)}
    first = count - 2
    sent = add([sums.pop(first)[0], swap(produced[first + 1], 1)]).astype(bf16)
    sent, *others = tie(sent, *[produced[r + 1] for r in sums])
    arrived = swap(sent, bits[1])
    for r, value in zip(sums, others):
        sums[r].append(swap(value, 1))
    early = (first - 2, first - 4)
    before, *held = tie(sent, *[sums[r][1] for r in early])
    for r, value in zip(early, held):
        sums[r][1] = value
    context = attention(before, 0)
    arrived, context = tie(arrived, context)
    sums[first ^ bits[1]].append(arrived)
    for r in range(first - 2, 0, -4):
        pair = tie(*[add(sums.pop(q)).astype(bf16) for q in (r, r - 2)])
        for q, value in zip((r, r - 2), pair):
            sums[q ^ low_bit(q)].append(swap(value, low_bit(q)))
    later = attention(pair[1], 1)
    context = jnp.concatenate([context, later]).reshape(rows, HEADS * HEAD)
    return (context, add(sums[0]).astype(bf16))


def solution(mesh):
    return jax.shard_map(
        shards,
        mesh=mesh,
        in_specs=(
            P(("grp", "ep"), None),
            P(("grp", "ep"), None, None),
            P(("grp", "ep"), None, None, None),
            P(("grp", "ep")),
            P(("grp", "ep"), None),
            P(),
            P(("grp", "ep"), None),
            P(("grp", "ep"), None),
            P("ep", None, None),
            P("ep", None, None),
            P("ep", None, None),
            P("ep", None, None),
            P("ep", None, None),
            P("ep", None, None, None),
            P("ep", None, None),
            P("ep", None, None),
        ),
        out_specs=(P(("grp", "ep"), None), P(("grp", "ep"), None)),
        check_vma=False,
    )
```
